128 devices in a mesh: node: 16 (over x_lo, z, core), group: 8 (over x_hi, y).
Axes of the slice: x: 4 (x_hi: 2, x_lo: 2; x = x_hi * 2 + x_lo), y: 4, z: 4, core: 2. Of those that a mesh axis runs over, the one named last changes fastest.
Arguments:
- queries: bfloat16 [65536, 1024], P(('group', 'node')), may hold values from -10 to 10, as said below
- key_rows: bfloat16 [65536, 1024], P(('group', 'node')), may hold values from -10 to 10, as said below
- value_rows: bfloat16 [65536, 1024], P(('group', 'node')), may hold values from -10 to 10, as said below
- grad_output: bfloat16 [65536, 2048], P(('group', 'node')), may hold values from -6 to 6
- out_weight: bfloat16 [1024, 2048], replicated, may hold values from -0.1875 to 0.1875
Outputs:
- grad_queries: bfloat16 [65536, 1024], P(('group', 'node'))
- grad_keys: bfloat16 [65536, 1024], P(('group', 'node'))
- grad_values: bfloat16 [65536, 1024], P(('group', 'node'))
- grad_weight: float32 [1024, 2048], replicated
The draws below stay inside these ranges and needn't reach their ends.
Inputs may be any that keep to these rules, and one draw needn't show every extreme that they name: `queries`: entries of order one. `key_rows`: entries of order one. `value_rows`: entries of order one.
All inputs are finite; a program needn't handle non-finite values.
Results may differ from the reference program's by a relative error of at most 0.018.
Values may be sent and summed in bfloat16 or wider, within the bound.
A program may use at most 128 MiB of HBM per device.

```python
import math
import jax
import jax.numpy as jnp
from jax import lax

D = 2048
HEADS = 8
HEAD_DIM = 128
LEAF = 128
S1 = 16
S2 = 256
TOK_DEV = 512
ATT_WIDTH = 1024
TOKENS = 65536
N_NODE = 16
N_GROUP = 8


def base_rows(key):
    width = HEADS * HEAD_DIM
    return jax.random.truncated_normal(jax.random.fold_in(key, 31), -4.0, 4.0, (TOKENS, width), jnp.float32)


def shared_rows(key):
    width = HEADS * HEAD_DIM
    span_key = jax.random.fold_in(key, 53)
    block_key = jax.random.fold_in(key, 59)
    span_part = jax.random.truncated_normal(span_key, -3.0, 3.0, (TOKENS // S2, width), jnp.float32)
    block_part = jax.random.truncated_normal(block_key, -3.0, 3.0, (TOKENS // S1, width), jnp.float32) * 0.5
    return jnp.repeat(span_part, S2, axis=0) + jnp.repeat(block_part, S1, axis=0)


def draw_queries(key, part):
    result = base_rows(jax.random.fold_in(key, 3))
    return result.astype(jnp.bfloat16)


def draw_key_rows(key, part):
    result = base_rows(jax.random.fold_in(key, 5)) + shared_rows(jax.random.fold_in(key, 41))
    return result.astype(jnp.bfloat16)


def draw_value_rows(key, part):
    result = base_rows(jax.random.fold_in(key, 7)) + shared_rows(jax.random.fold_in(key, 43))
    return result.astype(jnp.bfloat16)


def shard_levels(rng, dims, shards, low, high):
    level, own = 1.0, jax.random.fold_in(rng, 6)
    for axis_at, blocks in shards:
        draws = jnp.exp(jax.random.uniform(jax.random.fold_in(own, axis_at), (blocks,), jnp.float32, low / len(shards), high / len(shards)))
        level = level * jnp.repeat(draws, dims[axis_at] // blocks).reshape([-1 if axis == axis_at else 1 for axis in range(len(dims))])
    return level


def centred(rng, extent, scale, limit, pieces=(), kind=jnp.bfloat16):
    entries = jax.random.normal(rng, extent, jnp.float32) * scale
    if len(pieces) > 0:
        entries = shard_levels(rng, extent, pieces, -0.22, 0.18) * entries
    return jnp.clip(entries, min=-limit, max=limit).astype(kind)


def setup_inputs(seed: int = 0) -> dict:
    arg_keys = jax.random.split(jax.random.key(seed), 6)
    queries = draw_queries(jax.random.fold_in(arg_keys[5], 71), 0)
    key_rows = draw_key_rows(jax.random.fold_in(arg_keys[5], 71), 0)
    value_rows = draw_value_rows(jax.random.fold_in(arg_keys[5], 71), 0)
    grad_output = centred(arg_keys[3], (TOKENS, D), 1.0, 6.0, ((0, 128),))
    out_weight = centred(arg_keys[4], (ATT_WIDTH, D), ATT_WIDTH ** -0.5, 0.1875)
    return {"queries": queries, "key_rows": key_rows, "value_rows": value_rows, "grad_output": grad_output, "out_weight": out_weight}


NEG = -1e+30

def coarsen(array, factor):
    width = array.shape[1]
    summed = lax.optimization_barrier(jnp.mean(array.astype(jnp.float32).reshape(array.shape[0] // factor, factor, width), axis=1))
    return summed.astype(jnp.bfloat16)

def attend(query_blk, key_blk, value_blk, grad_blk, weight, near_keys, near_values, near_keep, far_keys, far_values, far_keep):
    row_count = query_blk.shape[0]
    head_count = HEADS
    head_width = HEAD_DIM
    pair_len = 2 * LEAF
    pair_count = row_count // pair_len
    inv_root = 1.0 / math.sqrt(head_width)

    def to_pairs(array):
        return array.astype(jnp.float32).reshape(pair_count, pair_len, head_count, head_width)

    def to_heads(array):
        return array.astype(jnp.float32).reshape(array.shape[0], head_count, head_width)
    query_pair = to_pairs(query_blk)
    key_pair = to_pairs(key_blk)
    value_pair = to_pairs(value_blk)
    query_head = to_heads(query_blk)
    near_key_head = to_heads(near_keys)
    near_value_head = to_heads(near_values)
    far_key_head = to_heads(far_keys)
    far_value_head = to_heads(far_values)
    fine_score = jnp.einsum('pqhd,pkhd->hpqk', query_pair, key_pair).reshape(head_count, row_count, pair_len) * inv_root
    near_score = jnp.where(near_keep[None], jnp.einsum('rhd,jhd->hrj', query_head, near_key_head) * inv_root, NEG)
    far_score = jnp.where(far_keep[None], jnp.einsum('rhd,jhd->hrj', query_head, far_key_head) * inv_root, NEG)
    row_max = jnp.maximum(jnp.maximum(fine_score.max(-1), near_score.max(-1)), far_score.max(-1))
    fine_exp = jnp.exp(fine_score - row_max[..., None])
    near_exp = jnp.exp(near_score - row_max[..., None])
    far_exp = jnp.exp(far_score - row_max[..., None])
    row_sum = fine_exp.sum(-1) + near_exp.sum(-1) + far_exp.sum(-1)
    fine_prob = fine_exp / row_sum[..., None]
    near_prob = near_exp / row_sum[..., None]
    far_prob = far_exp / row_sum[..., None]
    fine_low = fine_prob.astype(jnp.bfloat16).astype(jnp.float32).reshape(head_count, pair_count, pair_len, pair_len)
    near_low = near_prob.astype(jnp.bfloat16).astype(jnp.float32)
    far_low = far_prob.astype(jnp.bfloat16).astype(jnp.float32)
    fine_out = jnp.einsum('hpqk,pkhd->pqhd', fine_low, value_pair).reshape(row_count, head_count, head_width)
    near_out = jnp.einsum('hrj,jhd->rhd', near_low, near_value_head)
    far_out = jnp.einsum('hrj,jhd->rhd', far_low, far_value_head)
    attended = (fine_out + near_out + far_out).reshape(row_count, head_count * head_width).astype(jnp.bfloat16)
    grad_attended = lax.dot_general(grad_blk, weight, (((1,), (1,)), ((), ())), preferred_element_type=jnp.float32).astype(jnp.bfloat16)
    weight_part = lax.dot_general(attended, grad_blk, (((0,), (0,)), ((), ())), preferred_element_type=jnp.float32)
    row_delta = lax.optimization_barrier(jnp.sum(to_heads(attended) * to_heads(grad_attended), axis=-1)).T
    grad_pair = to_pairs(grad_attended)
    grad_head = to_heads(grad_attended)
    fine_dprob = jnp.einsum('pqhd,pkhd->hpqk', grad_pair, value_pair).reshape(head_count, row_count, pair_len)
    near_dprob = jnp.einsum('rhd,jhd->hrj', grad_head, near_value_head)
    far_dprob = jnp.einsum('rhd,jhd->hrj', grad_head, far_value_head)
    fine_dscore = (fine_prob * (fine_dprob - row_delta[..., None])).astype(jnp.bfloat16).astype(jnp.float32)
    near_dscore = (near_prob * (near_dprob - row_delta[..., None])).astype(jnp.bfloat16).astype(jnp.float32)
    far_dscore = (far_prob * (far_dprob - row_delta[..., None])).astype(jnp.bfloat16).astype(jnp.float32)
    fine_dfour = fine_dscore.reshape(head_count, pair_count, pair_len, pair_len)
    grad_query = jnp.einsum('hpqk,pkhd->pqhd', fine_dfour, key_pair).reshape(row_count, head_count, head_width)
    grad_query = grad_query + jnp.einsum('hrj,jhd->rhd', near_dscore, near_key_head)
    grad_query = grad_query + jnp.einsum('hrj,jhd->rhd', far_dscore, far_key_head)
    grad_query = (grad_query * inv_root).reshape(row_count, -1).astype(jnp.bfloat16)
    fine_dkey = (jnp.einsum('hpqk,pqhd->pkhd', fine_dfour, query_pair) * inv_root).reshape(row_count, -1)
    fine_dvalue = jnp.einsum('hpqk,pqhd->pkhd', fine_low, grad_pair).reshape(row_count, -1)
    near_dkey = (jnp.einsum('hrj,rhd->jhd', near_dscore, query_head) * inv_root).reshape(near_keys.shape[0], -1)
    near_dvalue = jnp.einsum('hrj,rhd->jhd', near_low, grad_head).reshape(near_keys.shape[0], -1)
    far_dkey = (jnp.einsum('hrj,rhd->jhd', far_dscore, query_head) * inv_root).reshape(far_keys.shape[0], -1)
    far_dvalue = jnp.einsum('hrj,rhd->jhd', far_low, grad_head).reshape(far_keys.shape[0], -1)
    return (grad_query, fine_dkey, fine_dvalue, near_dkey, near_dvalue, far_dkey, far_dvalue, weight_part)

def reference(queries, key_rows, value_rows, grad_output, out_weight):
    ratio = S2 // S1
    width = HEADS * HEAD_DIM
    near_keys = coarsen(key_rows, S1)
    near_values = coarsen(value_rows, S1)
    far_keys = coarsen(near_keys, ratio)
    far_values = coarsen(near_values, ratio)
    group_nearby = N_NODE * TOK_DEV // S1
    group_far = N_NODE * TOK_DEV // S2
    far_group = jnp.arange(far_keys.shape[0], dtype=jnp.int32) // group_far
    near_index = jnp.arange(group_nearby, dtype=jnp.int32)
    local_rows = jnp.arange(TOK_DEV, dtype=jnp.int32)

    def block_step(carried_state, block_id):
        nearby_key_accum, nearby_value_accum, distant_key_accum, distant_value_accum, weight_running_sum = carried_state
        node_id = block_id % N_NODE
        group_id = block_id // N_NODE
        row_start = (block_id * TOK_DEV).astype(jnp.int32)
        nearby_begin = (group_id * group_nearby).astype(jnp.int32)

        def gather_rows(array):
            return lax.dynamic_slice_in_dim(array, row_start, TOK_DEV, 0)
        group_keys = lax.dynamic_slice_in_dim(near_keys, nearby_begin, group_nearby, 0)
        group_values = lax.dynamic_slice_in_dim(near_values, nearby_begin, group_nearby, 0)
        position = node_id * TOK_DEV + local_rows
        near_keep = near_index[None, :] * S1 // (2 * LEAF) != position[:, None] // (2 * LEAF)
        far_keep = (far_group != group_id)[None, :]
        loop_outputs = attend(gather_rows(queries), gather_rows(key_rows), gather_rows(value_rows), gather_rows(grad_output), out_weight, group_keys, group_values, near_keep, far_keys, far_values, far_keep)
        nearby_key_accum = lax.dynamic_update_slice_in_dim(nearby_key_accum, lax.dynamic_slice_in_dim(nearby_key_accum, nearby_begin, group_nearby, 0) + loop_outputs[3], nearby_begin, 0)
        nearby_value_accum = lax.dynamic_update_slice_in_dim(nearby_value_accum, lax.dynamic_slice_in_dim(nearby_value_accum, nearby_begin, group_nearby, 0) + loop_outputs[4], nearby_begin, 0)
        distant_key_accum = distant_key_accum + loop_outputs[5]
        distant_value_accum = distant_value_accum + loop_outputs[6]
        weight_running_sum = weight_running_sum + loop_outputs[7]
        return ((nearby_key_accum, nearby_value_accum, distant_key_accum, distant_value_accum, weight_running_sum), (loop_outputs[0], loop_outputs[1], loop_outputs[2]))
    initial = (jnp.zeros((TOKENS // S1, width), jnp.float32), jnp.zeros((TOKENS // S1, width), jnp.float32), jnp.zeros((TOKENS // S2, width), jnp.float32), jnp.zeros((TOKENS // S2, width), jnp.float32), jnp.zeros((width, D), jnp.float32))
    final, stacked = lax.scan(block_step, initial, jnp.arange(N_NODE * N_GROUP, dtype=jnp.int32))
    grad_queries = stacked[0].reshape(TOKENS, width)
    near_key_total = final[0] + jnp.repeat(final[2] / ratio, ratio, axis=0)
    near_value_total = final[1] + jnp.repeat(final[3] / ratio, ratio, axis=0)
    grad_keys = (stacked[1].reshape(TOKENS, width) + jnp.repeat(near_key_total / S1, S1, axis=0)).astype(jnp.bfloat16)
    grad_values = (stacked[2].reshape(TOKENS, width) + jnp.repeat(near_value_total / S1, S1, axis=0)).astype(jnp.bfloat16)
    grad_weight = final[4] * (1.0 / math.sqrt(TOKENS))
    return (grad_queries, grad_keys, grad_values, grad_weight)
```

```python
import math

import jax
import jax.numpy as jnp
from jax import lax
from jax.experimental import pallas as pl
from jax.experimental.pallas import tpu as pltpu
from jax.sharding import PartitionSpec as P

HEADS = 8
WIDTH = 128
S1 = 16
ROWS = 512
PAIR = 256
CHIPS = 8
SLOT = 48
KEYS = 768
COLS = 2048
CLASSES = ((0, 3), (3, 3), (6, 2))
BF = jnp.bfloat16
F32 = jnp.float32
SCALE = 1.0 / math.sqrt(WIDTH)
EXP2_SCALE = math.log2(math.e) / math.sqrt(WIDTH)


def dot(a, b, ca, cb):
    return lax.dot_general(a, b, (((ca,), (cb,)), ((), ())), preferred_element_type=F32)


def flip4(a, d):
    if d == 0:
        return a
    if d == 1:
        return a + 1 - 2 * (a % 2)
    if d == 2:
        return (a + 2) % 4
    return 3 - a


def flip2(a, d):
    return 1 - a if d else a


class Place:
    def __init__(self):
        node = lax.axis_index("node")
        group = lax.axis_index("group")
        self.node, self.group = node, group
        self.core = node % 2
        self.z = (node // 2) % 4
        self.x_lo = node // 8
        self.x_hi = group // 4
        self.y = group % 4

    def coord(self, axis):
        return (self.x_hi * 2 + self.x_lo, self.y, self.z)[axis]

    def at(self, x_lo, x_hi, y, z, core):
        return {"node": (x_lo * 4 + z) * 2 + core, "group": x_hi * 4 + y}

    def sibling(self):
        return self.at(self.x_lo, self.x_hi, self.y, self.z, 1 - self.core)

    def chip(self, c):
        return self.at(
            flip2(self.x_lo, c // 4), self.x_hi, self.y, flip4(self.z, c % 4), self.core
        )

    def peer_group(self, j):
        return self.at(
            self.x_lo, flip2(self.x_hi, j // 4), flip4(self.y, j % 4), self.z, self.core
        )

    def along(self, axis, d):
        if axis == 0:
            return self.at(
                flip2(self.x_lo, d % 2), flip2(self.x_hi, d // 2), self.y, self.z, self.core
            )
        if axis == 1:
            return self.at(self.x_lo, self.x_hi, flip4(self.y, d), self.z, self.core)
        return self.at(self.x_lo, self.x_hi, self.y, flip4(self.z, d), self.core)


def send(src, dst, send_sem, recv_sem, device):
    copy = pltpu.make_async_remote_copy(
        src_ref=src,
        dst_ref=dst,
        send_sem=send_sem,
        recv_sem=recv_sem,
        device_id=device,
        device_id_type=pl.DeviceIdType.MESH,
    )
    copy.start()
    return copy


def kernel(
    q_ref, k_ref, v_ref, go_ref, w_ref,
    gq_ref, gk_ref, gv_ref, wout,
    nf, fx_send, fx, far_blk, gt, att, probs, gst, gs, delta,
    gnf, cr, snd, rr, fine_k, fine_v, tot, fb_send, fb,
    wpart, wr0, ra, rb, rc, sa, sb,
    near_ss, near_rs, far_ss, far_rs, fx_ss, fx_rs,
    g_ss, g_rs, w_ss, w_rs, core_ss, core_rs, fb_ss, fb_rs,
):
    me = Place()
    core = me.core

    barrier = pltpu.get_barrier_semaphore()
    partners = [me.sibling()]
    partners += [me.chip(c) for c in range(1, CHIPS)]
    partners += [me.peer_group(j) for j in range(1, 8)]
    partners += [me.along(0, 3)]
    for partner in partners:
        pl.semaphore_signal(barrier, inc=1, device_id=partner, device_id_type=pl.DeviceIdType.MESH)

    rows = lax.broadcasted_iota(jnp.int32, (32, ROWS), 0)
    toks = lax.broadcasted_iota(jnp.int32, (32, ROWS), 1)
    mean16 = jnp.where(toks // S1 == rows, 1.0 / S1, 0.0).astype(BF)
    near_k = dot(mean16, k_ref[...], 1, 0).astype(BF)
    near_v = dot(mean16, v_ref[...], 1, 0).astype(BF)
    nf[0, 0:32, :] = near_k
    nf[1, 0:32, :] = near_v
    r8 = lax.broadcasted_iota(jnp.int32, (8, 32), 0)
    c8 = lax.broadcasted_iota(jnp.int32, (8, 32), 1) // 16
    pick_k = jnp.where(c8 == r8, 1.0 / S1, 0.0).astype(BF)
    pick_v = jnp.where(c8 + 2 == r8, 1.0 / S1, 0.0).astype(BF)
    far_own = (dot(pick_k, near_k, 1, 0) + dot(pick_v, near_v, 1, 0)).astype(BF).astype(F32)
    fx_send[...] = far_own

    pl.semaphore_wait(barrier, len(partners))

    fx_copies = []
    for j in range(1, 8):
        fx_copies.append(
            send(fx_send, fx.at[j], fx_ss.at[j], fx_rs.at[j], me.peer_group(j))
        )
    near_copies = [None]
    for c in range(1, CHIPS):
        near_copies.append(
            send(
                nf.at[:, pl.ds(0, 32), :],
                nf.at[:, pl.ds(SLOT * c, 32), :],
                near_ss.at[c],
                near_rs.at[c],
                me.chip(c),
            )
        )
    near_fwd = [
        send(
            nf.at[:, pl.ds(0, 32), :],
            nf.at[:, pl.ds(SLOT * CHIPS, 32), :],
            near_ss.at[CHIPS],
            near_rs.at[CHIPS],
            me.sibling(),
        )
    ]

    def project(i, carry):
        r = pl.ds(pl.multiple_of(i * 256, 256), 256)
        gt[r, :] = dot(w_ref[r, :], go_ref[...], 1, 1).astype(BF)
        return carry

    lax.fori_loop(0, 4, project, 0)

    for j in range(1, 8):
        fx_copies[j - 1].wait()
    far_blk[0, 0:2, :] = far_own[0:2]
    far_blk[1, 0:2, :] = far_own[2:4]
    for j in range(1, 8):
        far_blk[0, 2 * j : 2 * j + 2, :] = fx[j, 0:2, :]
        far_blk[1, 2 * j : 2 * j + 2, :] = fx[j, 2:4, :]
    nf[:, 32:48, :] = far_blk[...].astype(BF)
    far_copies = [None]
    for c in range(1, CHIPS):
        far_copies.append(
            send(
                nf.at[:, pl.ds(32, 16), :],
                nf.at[:, pl.ds(SLOT * c + 32, 16), :],
                far_ss.at[c],
                far_rs.at[c],
                me.chip(c),
            )
        )
    far_fwd = [
        send(
            nf.at[:, pl.ds(32, 16), :],
            nf.at[:, pl.ds(SLOT * CHIPS + 32, 16), :],
            far_ss.at[CHIPS],
            far_rs.at[CHIPS],
            me.sibling(),
        )
    ]
    for c in range(1, CHIPS):
        near_copies[c].wait()
        near_fwd.append(
            send(
                nf.at[:, pl.ds(SLOT * c, 32), :],
                nf.at[:, pl.ds(SLOT * (CHIPS + c), 32), :],
                near_ss.at[CHIPS + c],
                near_rs.at[CHIPS + c],
                me.sibling(),
            )
        )
    for c in range(1, CHIPS):
        far_copies[c].wait()
        far_fwd.append(
            send(
                nf.at[:, pl.ds(SLOT * c + 32, 16), :],
                nf.at[:, pl.ds(SLOT * (CHIPS + c) + 32, 16), :],
                far_ss.at[CHIPS + c],
                far_rs.at[CHIPS + c],
                me.sibling(),
            )
        )
    for c in range(CHIPS):
        near_fwd[c].wait()
        far_fwd[c].wait()

    row = lax.broadcasted_iota(jnp.int32, (KEYS, ROWS), 0)
    col = lax.broadcasted_iota(jnp.int32, (KEYS, ROWS), 1)
    hidden = (row % SLOT >= 32) & (row % SLOT < 34)
    hidden = hidden | ((row < 32) & (row // S1 == col // PAIR))

    def forward(h, carry):
        c = pl.ds(pl.multiple_of(h * WIDTH, WIDTH), WIDTH)
        qh = q_ref[:, c]
        s = dot(nf[0, :, c], qh, 1, 1)
        sf = [
            dot(k_ref[p * PAIR : (p + 1) * PAIR, c], qh[p * PAIR : (p + 1) * PAIR], 1, 1)
            for p in range(2)
        ]
        sf = jnp.concatenate(sf, axis=1)
        top = jnp.maximum(jnp.max(s, axis=0, keepdims=True), jnp.max(sf, axis=0, keepdims=True))
        e = jnp.exp2((s - top) * EXP2_SCALE)
        e = jnp.where(hidden, 0.0, e)
        ef = jnp.exp2((sf - top) * EXP2_SCALE)
        total = jnp.sum(e, axis=0, keepdims=True) + jnp.sum(ef, axis=0, keepdims=True)
        e = e.astype(BF)
        ef = ef.astype(BF)
        probs[h, 0:KEYS, :] = e
        probs[h, KEYS : KEYS + PAIR, :] = ef
        out = dot(nf[1, :, c], e, 0, 0)
        of = [
            dot(v_ref[p * PAIR : (p + 1) * PAIR, c], ef[:, p * PAIR : (p + 1) * PAIR], 0, 0)
            for p in range(2)
        ]
        out = out + jnp.concatenate(of, axis=1)
        inv = 1.0 / total
        out = (out * inv).astype(BF)
        att[c, :] = out
        gth = gt[c, :].astype(F32)
        d = jnp.sum(out.astype(F32) * gth, axis=0, keepdims=True) * inv
        delta[h] = jnp.broadcast_to(d, (8, ROWS))
        scaled = gth * inv
        gst[c, :] = scaled.astype(BF)
        gs[:, c] = scaled.T.astype(BF)
        return carry

    lax.fori_loop(0, HEADS, forward, 0)

    def weigh(i, carry):
        c = pl.ds(pl.multiple_of(i * 512, 512), 512)
        part = dot(att[...], go_ref[:, c], 1, 0)
        wpart[:, :, c] = part.reshape(HEADS, WIDTH, 512).astype(BF)
        return carry

    lax.fori_loop(0, 4, weigh, 0)

    def backward(h, carry):
        c = pl.ds(pl.multiple_of(h * WIDTH, WIDTH), WIDTH)
        qh = q_ref[:, c]
        gth = gst[c, :]
        gh = gs[:, c]
        d = delta[h, 0:1, :]
        kk = nf[0, :, c]
        e = probs[h, 0:KEYS, :]
        ds = (e.astype(F32) * (dot(nf[1, :, c], gth, 1, 0) - d)).astype(BF)
        gnf[1, :, c] = dot(e, gh, 1, 0).astype(BF)
        gnf[0, :, c] = (dot(ds, qh, 1, 0) * SCALE).astype(BF)
        dq = dot(kk, ds, 0, 0)
        dqf = []
        for p in range(2):
            r = slice(p * PAIR, (p + 1) * PAIR)
            ef = probs[h, KEYS : KEYS + PAIR, r]
            dsf = (ef.astype(F32) * (dot(v_ref[r, c], gth[:, r], 1, 0) - d[:, r])).astype(BF)
            fine_v[r, c] = dot(ef, gh[r], 1, 0)
            fine_k[r, c] = dot(dsf, qh[r], 1, 0) * SCALE
            dqf.append(dot(k_ref[r, c], dsf, 0, 0))
        dq = (dq + jnp.concatenate(dqf, axis=1)) * SCALE
        gq_ref[:, c] = dq.T.astype(BF)
        return carry

    lax.fori_loop(0, HEADS, backward, 0)

    half = CHIPS * SLOT
    to_sib = send(
        gnf.at[:, pl.ds(half, half), :], cr, core_ss.at[0], core_rs.at[0], me.sibling()
    )
    mine = pl.multiple_of(core * 64, 64)
    other = pl.multiple_of((1 - core) * 64, 64)
    w_sib = send(
        wpart.at[:, pl.ds(other, 64), :], wr0, core_ss.at[1], core_rs.at[1], me.sibling()
    )
    w_sib.wait()

    def add_core(h, carry):
        r = pl.ds(mine, 64)
        wpart[h, r, :] = (wpart[h, r, :].astype(F32) + wr0[h].astype(F32)).astype(BF)
        return carry

    lax.fori_loop(0, HEADS, add_core, 0)

    order = [[(cls + step) % 3 for step in range(3)] for cls in range(3)]

    def xor_coord(axis, d):
        if axis == 0:
            return flip2(me.x_hi, d // 2) * 2 + flip2(me.x_lo, d % 2)
        return flip4(me.coord(axis), d)

    def rs_a(cls):
        h0, hn = CLASSES[cls]
        axis = order[cls][0]
        return [
            send(
                wpart.at[
                    pl.ds(h0, hn), pl.ds(pl.multiple_of(mine + xor_coord(axis, d) * 16, 16), 16), :
                ],
                ra.at[d - 1, pl.ds(h0, hn)],
                w_ss.at[0, cls, d - 1],
                w_rs.at[0, cls, d - 1],
                me.along(axis, d),
            )
            for d in range(1, 4)
        ]

    def rs_b(cls):
        h0, hn = CLASSES[cls]
        axis = order[cls][1]
        return [
            send(
                sa.at[
                    pl.ds(h0, hn), :, pl.ds(pl.multiple_of(xor_coord(axis, d) * 512, 512), 512)
                ],
                rb.at[d - 1, pl.ds(h0, hn)],
                w_ss.at[1, cls, d - 1],
                w_rs.at[1, cls, d - 1],
                me.along(axis, d),
            )
            for d in range(1, 4)
        ]

    def rs_c(cls):
        h0, hn = CLASSES[cls]
        axis = order[cls][2]
        return [
            send(
                sb.at[
                    pl.ds(h0, hn), :, pl.ds(pl.multiple_of(xor_coord(axis, d) * 128, 128), 128)
                ],
                rc.at[d - 1, pl.ds(h0, hn)],
                w_ss.at[2, cls, d - 1],
                w_rs.at[2, cls, d - 1],
                me.along(axis, d),
            )
            for d in range(1, 4)
        ]

    def spot(cls):
        a, b, c = [me.coord(axis) for axis in order[cls]]
        return (
            pl.multiple_of(mine + a * 16, 16),
            pl.multiple_of(b * 512, 512),
            pl.multiple_of(b * 512 + c * 128, 128),
        )

    def gather(cls, step):
        h0, hn = CLASSES[cls]
        hs = pl.ds(h0, hn)
        row0, col_b, col_c = spot(cls)
        if step == 2:
            piece = wout.at[hs, pl.ds(row0, 16), pl.ds(col_c, 128)]
        elif step == 1:
            piece = wout.at[hs, pl.ds(row0, 16), pl.ds(col_b, 512)]
        else:
            piece = wout.at[hs, pl.ds(row0, 16), :]
        axis = order[cls][step]
        return [
            send(
                piece, piece, w_ss.at[5 - step, cls, d - 1], w_rs.at[5 - step, cls, d - 1],
                me.along(axis, d),
            )
            for d in range(1, 4)
        ]

    copies = [rs_a(cls) for cls in range(3)]

    to_sib.wait()
    for i in range(2):
        snd[i] = (gnf[i, 0:half, :].astype(F32) + cr[i].astype(F32)).astype(BF)
    near_rs_copies = []
    for c in range(1, CHIPS):
        near_rs_copies.append(
            send(
                snd.at[:, pl.ds(SLOT * c, SLOT), :],
                rr.at[c],
                g_ss.at[c],
                g_rs.at[c],
                me.chip(c),
            )
        )

    next_copies = []
    for cls in range(3):
        h0, hn = CLASSES[cls]
        for copy in copies[cls]:
            copy.wait()
        row0, _, _ = spot(cls)
        for h in range(h0, h0 + hn):
            t = wpart[h, pl.ds(row0, 16), :].astype(F32)
            for d in range(3):
                t = t + ra[d, h].astype(F32)
            sa[h] = t.astype(BF)
        next_copies.append(rs_b(cls))
    copies, next_copies = next_copies, []
    for cls in range(3):
        h0, hn = CLASSES[cls]
        for copy in copies[cls]:
            copy.wait()
        _, col_b, _ = spot(cls)
        hs = slice(h0, h0 + hn)
        t = sa[hs, :, pl.ds(col_b, 512)].astype(F32)
        for d in range(3):
            t = t + rb[d, hs].astype(F32)
        sb[hs] = t.astype(BF)
        next_copies.append(rs_c(cls))
    copies, next_copies = next_copies, []
    for cls in range(3):
        h0, hn = CLASSES[cls]
        for copy in copies[cls]:
            copy.wait()
        row0, _, col_c = spot(cls)
        hs = slice(h0, h0 + hn)
        c0 = pl.multiple_of(me.coord(order[cls][2]) * 128, 128)
        t = sb[hs, :, pl.ds(c0, 128)].astype(F32)
        for d in range(3):
            t = t + rc[d, hs].astype(F32)
        wout[hs, pl.ds(row0, 16), pl.ds(col_c, 128)] = t.astype(BF)
        next_copies.append(gather(cls, 2))
    copies, next_copies = next_copies, []

    for c in range(1, CHIPS):
        near_rs_copies[c - 1].wait()
    for i in range(2):
        t = snd[i, 0:SLOT, :].astype(F32)
        for c in range(1, CHIPS):
            t = t + rr[c, i].astype(F32)
        tot[i] = t
    for j in range(1, 8):
        fb_send[j, 0:2, :] = tot[0, 32 + 2 * j : 34 + 2 * j, :]
        fb_send[j, 2:4, :] = tot[1, 32 + 2 * j : 34 + 2 * j, :]
        fb_send[j, 4:8, :] = jnp.zeros((4, HEADS * WIDTH), F32)
    far_back = [
        send(fb_send.at[j], fb.at[j], fb_ss.at[j], fb_rs.at[j], me.peer_group(j))
        for j in range(1, 8)
    ]

    for step in (1, 0):
        for cls in range(3):
            for copy in copies[cls]:
                copy.wait()
            next_copies.append(gather(cls, step))
        copies, next_copies = next_copies, []
    for cls in range(3):
        for copy in copies[cls]:
            copy.wait()
    piece = wout.at[:, pl.ds(mine, 64), :]
    last = send(piece, piece, core_ss.at[2], core_rs.at[2], me.sibling())

    for copy in far_back:
        copy.wait()
    far_sum = fb[1]
    for j in range(2, 8):
        far_sum = far_sum + fb[j]
    far_sum = far_sum * (1.0 / (S1 * S1))
    for i in range(2):
        for r in range(2):
            part = tot[i, 16 * r : 16 * r + 16, :] * (1.0 / S1)
            tot[i, 16 * r : 16 * r + 16, :] = part + far_sum[2 * i + r : 2 * i + r + 1, :]

    def finish(i, carry):
        r = pl.ds(pl.multiple_of(i * S1, S1), S1)
        gk_ref[r, :] = (fine_k[r, :] + tot[0, pl.ds(i, 1), :]).astype(BF)
        gv_ref[r, :] = (fine_v[r, :] + tot[1, pl.ds(i, 1), :]).astype(BF)
        return carry

    lax.fori_loop(0, ROWS // S1, finish, 0)
    last.wait()


def body(queries, key_rows, value_rows, grad_output, out_weight):
    width = HEADS * WIDTH
    vmem = pltpu.VMEM
    dma = pltpu.SemaphoreType.DMA
    scratch = [
        vmem((2, KEYS, width), BF),
        vmem((8, width), F32),
        vmem((8, 8, width), F32),
        vmem((2, 16, width), F32),
        vmem((width, ROWS), BF),
        vmem((width, ROWS), BF),
        vmem((HEADS, KEYS + PAIR, ROWS), BF),
        vmem((width, ROWS), BF),
        vmem((ROWS, width), BF),
        vmem((HEADS, 8, ROWS), F32),
        vmem((2, KEYS, width), BF),
        vmem((2, CHIPS * SLOT, width), BF),
        vmem((2, CHIPS * SLOT, width), BF),
        vmem((CHIPS, 2, SLOT, width), BF),
        vmem((ROWS, width), F32),
        vmem((ROWS, width), F32),
        vmem((2, SLOT, width), F32),
        vmem((8, 8, width), F32),
        vmem((8, 8, width), F32),
        vmem((HEADS, WIDTH, COLS), BF),
        vmem((HEADS, 64, COLS), BF),
        vmem((3, HEADS, 16, COLS), BF),
        vmem((3, HEADS, 16, 512), BF),
        vmem((3, HEADS, 16, 128), BF),
        vmem((HEADS, 16, COLS), BF),
        vmem((HEADS, 16, 512), BF),
        dma((16,)), dma((16,)), dma((16,)), dma((16,)), dma((8,)), dma((8,)),
        dma((8,)), dma((8,)), dma((6, 3, 3)), dma((6, 3, 3)), dma((3,)), dma((3,)),
        dma((8,)), dma((8,)),
    ]
    spec = pl.BlockSpec(memory_space=pltpu.VMEM)
    gq, gk, gv, weight = pl.pallas_call(
        kernel,
        out_shape=(
            jax.ShapeDtypeStruct((ROWS, width), BF),
            jax.ShapeDtypeStruct((ROWS, width), BF),
            jax.ShapeDtypeStruct((ROWS, width), BF),
            jax.ShapeDtypeStruct((HEADS, WIDTH, COLS), BF),
        ),
        in_specs=[spec] * 5,
        out_specs=(spec,) * 4,
        scratch_shapes=scratch,
        compiler_params=pltpu.CompilerParams(
            collective_id=0, has_side_effects=True, vmem_limit_bytes=64 * 1024 * 1024 - 65536
        ),
        name="fused",
    )(queries, key_rows, value_rows, grad_output, out_weight)
    tokens = ROWS * lax.axis_size("node") * lax.axis_size("group")
    weight = weight.reshape(width, COLS).astype(F32) * (1.0 / math.sqrt(tokens))
    return gq, gk, gv, weight


def solution(mesh):
    split = P(("group", "node"), None)
    return jax.shard_map(
        body,
        mesh=mesh,
        in_specs=(split, split, split, split, P()),
        out_specs=(split, split, split, P()),
        check_vma=False,
    )
```

```python
import functools
import math

import jax
import jax.numpy as jnp
from jax import lax
from jax.experimental import pallas as pl
from jax.experimental.pallas import tpu as pltpu
from jax.sharding import PartitionSpec as P

HEADS = 8
WIDTH = 128
S1 = 16
ROWS = 512
PAIR = 256
CHIPS = 8
KEYS = 768
HALF = 384
FAR = 256
COLS = 2048
ALL = HEADS * WIDTH
UNITS = ((0, 3), (3, 3), (6, 2))
ORDERS = (
    (1, 0, 2), (0, 2, 1), (2, 1, 0), (1, 2, 0), (0, 1, 2), (2, 0, 1), (1, 0, 2), (1, 2, 0),
)
NSEM = 288
BF = jnp.bfloat16
F32 = jnp.float32
SCALE = 1.0 / math.sqrt(WIDTH)
EXP2_SCALE = math.log2(math.e) / math.sqrt(WIDTH)


def dot(a, b, ca, cb):
    return lax.dot_general(a, b, (((ca,), (cb,)), ((), ())), preferred_element_type=F32)


def flip4(a, d):
    if d == 0:
        return a
    if d == 1:
        return a + 1 - 2 * (a % 2)
    if d == 2:
        return (a + 2) % 4
    return 3 - a


def flip2(a, d):
    return 1 - a if d else a


class Place:
    def __init__(self):
        node = lax.axis_index("node")
        group = lax.axis_index("group")
        self.node, self.group = node, group
        self.core = node % 2
        self.z = (node // 2) % 4
        self.x_lo = node // 8
        self.x_hi = group // 4
        self.y = group % 4

    def coord(self, axis):
        return (self.x_hi * 2 + self.x_lo, self.y, self.z)[axis]

    def at(self, x_lo, x_hi, y, z, core):
        return {"node": (x_lo * 4 + z) * 2 + core, "group": x_hi * 4 + y}

    def sibling(self):
        return self.at(self.x_lo, self.x_hi, self.y, self.z, 1 - self.core)

    def chip(self, c):
        return self.at(
            flip2(self.x_lo, c // 4), self.x_hi, self.y, flip4(self.z, c % 4), self.core
        )

    def peer_group(self, j):
        return self.at(
            self.x_lo, flip2(self.x_hi, j // 4), flip4(self.y, j % 4), self.z, self.core
        )

    def coord_flip(self, axis, d):
        if axis == 0:
            return flip2(self.x_hi, d // 2) * 2 + flip2(self.x_lo, d % 2)
        return flip4(self.coord(axis), d)

    def along(self, axis, d):
        if axis == 0:
            return self.at(
                flip2(self.x_lo, d % 2), flip2(self.x_hi, d // 2), self.y, self.z, self.core
            )
        if axis == 1:
            return self.at(self.x_lo, self.x_hi, flip4(self.y, d), self.z, self.core)
        return self.at(self.x_lo, self.x_hi, self.y, flip4(self.z, d), self.core)


class Sems:
    def __init__(self, send_sems, recv_sems):
        self.send_sems, self.recv_sems, self.used = send_sems, recv_sems, 0

    def copy(self, src, dst, device):
        i = self.used
        self.used += 1
        return Copy(src, dst, self.send_sems.at[i], self.recv_sems.at[i], device)


class Copy:
    def __init__(self, src, dst, send_sem, recv_sem, device):
        self.parts = src, dst, send_sem, recv_sem, device

    def make(self):
        src, dst, send_sem, recv_sem, device = self.parts
        return pltpu.make_async_remote_copy(
            src_ref=src(),
            dst_ref=dst(),
            send_sem=send_sem,
            recv_sem=recv_sem,
            device_id=device(),
            device_id_type=pl.DeviceIdType.MESH,
        )

    def start(self):
        self.make().start()

    def wait(self):
        self.make().wait()


def start(copies):
    for copy in copies:
        copy.start()


def wait(copies):
    for copy in copies:
        copy.wait()


def kernel(
    q_hbm, k_hbm, v_hbm, go_hbm, w_hbm,
    gq_hbm, gk_hbm, gv_hbm, wout_hbm,
    q_ref, k_ref, v_ref, go_ref, w_ref,
    nf, zsend, zrecv, xblk, xsend, xrecv, gt, att, probs, gst, gs, delta,
    gnf, cr, snd, rr, yr, bxs, bxr, bzs, bzr, fine_k, fine_v, tot,
    wpart, wr0, ra, rb, rc, sa, sb, wout,
    load_sem, store_sem, send_sems, recv_sems,
):
    me = Place()
    core = me.core
    sems = Sems(send_sems, recv_sems)

    barrier = pltpu.get_barrier_semaphore()
    partners = [me.sibling()]
    partners += [me.chip(c) for c in range(1, CHIPS)]
    partners += [me.along(1, d) for d in range(1, 4)]
    partners += [me.along(0, d) for d in range(2, 4)]
    for partner in partners:
        pl.semaphore_signal(barrier, inc=1, device_id=partner, device_id_type=pl.DeviceIdType.MESH)

    loads = [
        pltpu.make_async_copy(src, dst, load_sem.at[i])
        for i, (src, dst) in enumerate(
            ((k_hbm, k_ref), (v_hbm, v_ref), (go_hbm, go_ref), (w_hbm, w_ref), (q_hbm, q_ref))
        )
    ]
    for load in loads:
        load.start()

    def near_at(c):
        return lambda: nf.at[:, pl.ds(32 * c, 32), :]

    def far_at(d):
        return lambda: nf.at[:, pl.ds(FAR + 32 * d, 32), :]

    def sib_at(first, rows):
        return lambda: nf.at[:, pl.ds(HALF + first, rows), :]

    z_gather = [
        sems.copy(lambda: zsend, lambda d=d: zrecv.at[d], lambda d=d: me.along(2, d))
        for d in range(1, 4)
    ]
    x_gather = [
        sems.copy(lambda: xsend, lambda d=d: xrecv.at[d], lambda d=d: me.along(0, d))
        for d in range(1, 4)
    ]
    y_gather = [
        sems.copy(far_at(0), far_at(d), lambda d=d: me.along(1, d)) for d in range(1, 4)
    ]
    near_gather = [
        sems.copy(near_at(0), near_at(c), lambda c=c: me.chip(c)) for c in range(1, CHIPS)
    ]
    near_forward = [
        sems.copy(near_at(c), sib_at(32 * c, 32), me.sibling) for c in range(CHIPS)
    ]
    far_forward = [
        sems.copy(far_at(d), sib_at(FAR + 32 * d, 32), me.sibling) for d in range(4)
    ]

    rows = lax.broadcasted_iota(jnp.int32, (32, ROWS), 0)
    toks = lax.broadcasted_iota(jnp.int32, (32, ROWS), 1)
    mean16 = jnp.where(toks // S1 == rows, 1.0 / S1, 0.0).astype(BF)
    r8 = lax.broadcasted_iota(jnp.int32, (8, 32), 0)
    c8 = lax.broadcasted_iota(jnp.int32, (8, 32), 1) // 16
    pick_k = jnp.where(c8 == r8, 1.0 / S1, 0.0).astype(BF)
    pick_v = jnp.where(c8 + 2 == r8, 1.0 / S1, 0.0).astype(BF)
    loads[0].wait()
    near_k = dot(mean16, k_ref[...], 1, 0).astype(BF)
    nf[0, 0:32, :] = near_k
    loads[1].wait()
    near_v = dot(mean16, v_ref[...], 1, 0).astype(BF)
    nf[1, 0:32, :] = near_v
    far_own = (dot(pick_k, near_k, 1, 0) + dot(pick_v, near_v, 1, 0)).astype(BF).astype(F32)
    zown = jnp.concatenate([far_own[0:4, 0 : ALL // 2], far_own[0:4, ALL // 2 :]], axis=0)
    zsend[...] = zown

    pl.semaphore_wait(barrier, len(partners))
    start(z_gather)
    start(near_gather)
    near_forward[0].start()

    def project(i, carry):
        r = pl.ds(pl.multiple_of(i * 256, 256), 256)
        gt[r, :] = dot(w_ref[r, :], go_ref[...], 1, 1).astype(BF)
        return carry

    loads[2].wait()
    loads[3].wait()
    lax.fori_loop(0, 2, project, 0)

    wait(z_gather)
    for d in range(4):
        block = zown if d == 0 else zrecv[d]
        for i in range(2):
            for part in range(2):
                xblk[8 * i + 2 * d : 8 * i + 2 * d + 2, part * 512 : part * 512 + 512] = block[
                    4 * part + 2 * i : 4 * part + 2 * i + 2
                ]
    xsend[...] = xblk[...].astype(BF)
    start(x_gather)
    lax.fori_loop(2, 4, project, 0)
    wait(x_gather)
    blocks = [xblk[...]] + [xrecv[d].astype(F32) for d in range(1, 4)]
    for i in range(2):
        nf[i, FAR : FAR + 32, :] = jnp.concatenate(
            [block[8 * i : 8 * i + 8] for block in blocks], axis=0
        ).astype(BF)
    start(y_gather)
    far_forward[0].start()
    loads[4].wait()
    for c in range(1, CHIPS):
        near_gather[c - 1].wait()
        near_forward[c].start()
    for d in range(1, 4):
        y_gather[d - 1].wait()
        far_forward[d].start()
    wait(near_forward)
    wait(far_forward)

    mine = pl.multiple_of(core * 64, 64)
    other = pl.multiple_of((1 - core) * 64, 64)

    def heads(u):
        return range(UNITS[u][0], UNITS[u][0] + UNITS[u][1])

    def span(u):
        return pl.ds(*UNITS[u])

    def columns(u):
        return pl.ds(UNITS[u][0] * WIDTH, UNITS[u][1] * WIDTH)

    def row_a(h, d=0):
        return pl.multiple_of(mine + me.coord_flip(ORDERS[h][0], d) * 16, 16)

    def col_b(h, d=0):
        return pl.multiple_of(me.coord_flip(ORDERS[h][1], d) * 512, 512)

    def col_c(h, d=0):
        return pl.multiple_of(me.coord_flip(ORDERS[h][2], d) * 128, 128)

    def piece(h, step):
        if step == 2:
            return wout.at[h, pl.ds(row_a(h), 16), pl.ds(col_b(h) + col_c(h), 128)]
        if step == 1:
            return wout.at[h, pl.ds(row_a(h), 16), pl.ds(col_b(h), 512)]
        return wout.at[h, pl.ds(row_a(h), 16), :]

    w_core, w_a, w_b, w_c, w_g, w_sib, w_out = [], [], [], [], [[], [], []], [], []
    for u in range(3):
        w_core.append(
            sems.copy(
                lambda u=u: wpart.at[span(u), pl.ds(other, 64), :],
                lambda u=u: wr0.at[span(u)],
                me.sibling,
            )
        )
        w_sib.append(
            sems.copy(
                lambda u=u: wout.at[span(u), pl.ds(mine, 64), :],
                lambda u=u: wout.at[span(u), pl.ds(mine, 64), :],
                me.sibling,
            )
        )
        w_out.append(
            pltpu.make_async_copy(wout.at[span(u)], wout_hbm.at[span(u)], store_sem.at[u])
        )
        w_a.append([
            sems.copy(
                lambda h=h, d=d: wpart.at[h, pl.ds(row_a(h, d), 16), :],
                lambda h=h, d=d: ra.at[d - 1, h],
                lambda h=h, d=d: me.along(ORDERS[h][0], d),
            )
            for h in heads(u) for d in range(1, 4)
        ])
        w_b.append([
            sems.copy(
                lambda h=h, d=d: sa.at[h, :, pl.ds(col_b(h, d), 512)],
                lambda h=h, d=d: rb.at[d - 1, h],
                lambda h=h, d=d: me.along(ORDERS[h][1], d),
            )
            for h in heads(u) for d in range(1, 4)
        ])
        w_c.append([
            sems.copy(
                lambda h=h, d=d: sb.at[h, :, pl.ds(col_c(h, d), 128)],
                lambda h=h, d=d: rc.at[d - 1, h],
                lambda h=h, d=d: me.along(ORDERS[h][2], d),
            )
            for h in heads(u) for d in range(1, 4)
        ])
        for step in range(3):
            w_g[step].append([
                sems.copy(
                    lambda h=h, step=step: piece(h, step),
                    lambda h=h, step=step: piece(h, step),
                    lambda h=h, d=d, step=step: me.along(ORDERS[h][step], d),
                )
                for h in heads(u) for d in range(1, 4)
            ])

    def weigh(u):
        def some(i, carry):
            c = pl.ds(pl.multiple_of(i * 512, 512), 512)
            part = dot(att[columns(u), :], go_ref[:, c], 1, 0)
            wpart[span(u), :, c] = part.reshape(UNITS[u][1], WIDTH, 512).astype(BF)
            return carry

        lax.fori_loop(0, COLS // 512, some, 0)
        w_core[u].start()

    def weight_core(u):
        w_core[u].wait()

        def some(h, carry):
            r = pl.ds(mine, 64)
            wpart[h, r, :] = (wpart[h, r, :].astype(F32) + wr0[h].astype(F32)).astype(BF)
            return carry

        lax.fori_loop(heads(u)[0], heads(u)[-1] + 1, some, 0)
        start(w_a[u])

    def weight_a(u):
        wait(w_a[u])
        for h in heads(u):
            t = wpart[h, pl.ds(row_a(h), 16), :].astype(F32)
            for d in range(3):
                t = t + ra[d, h].astype(F32)
            sa[h] = t.astype(BF)
        start(w_b[u])

    def weight_b(u):
        wait(w_b[u])
        for h in heads(u):
            t = sa[h, :, pl.ds(col_b(h), 512)].astype(F32)
            for d in range(3):
                t = t + rb[d, h].astype(F32)
            sb[h] = t.astype(BF)
        start(w_c[u])

    def weight_c(u):
        wait(w_c[u])
        for h in heads(u):
            t = sb[h, :, pl.ds(col_c(h), 128)].astype(F32)
            for d in range(3):
                t = t + rc[d, h].astype(F32)
            c = pl.multiple_of(col_b(h) + col_c(h), 128)
            wout[h, pl.ds(row_a(h), 16), pl.ds(c, 128)] = t.astype(BF)
        start(w_g[2][u])

    def weight_gather(u, step):
        wait(w_g[step][u])
        if step > 0:
            start(w_g[step - 1][u])
        else:
            w_sib[u].start()

    def weight_last(u):
        w_sib[u].wait()
        w_out[u].start()

    n_core, n_near, n_y, n_x, n_z = [], [], [], [], []
    for u in range(3):
        n_core.append(
            sems.copy(
                lambda u=u: gnf.at[:, pl.ds(HALF, HALF), columns(u)],
                lambda u=u: cr.at[:, :, columns(u)],
                me.sibling,
            )
        )
        n_near.append([
            sems.copy(
                lambda u=u, c=c: snd.at[:, pl.ds(32 * c, 32), columns(u)],
                lambda u=u, c=c: rr.at[c, :, :, columns(u)],
                lambda c=c: me.chip(c),
            )
            for c in range(1, CHIPS)
        ])
        n_y.append([
            sems.copy(
                lambda u=u, d=d: snd.at[:, pl.ds(FAR + 32 * d, 32), columns(u)],
                lambda u=u, d=d: yr.at[d, :, :, columns(u)],
                lambda d=d: me.along(1, d),
            )
            for d in range(1, 4)
        ])
        n_x.append([
            sems.copy(
                lambda u=u, d=d: bxs.at[d, :, columns(u)],
                lambda u=u, d=d: bxr.at[d, :, columns(u)],
                lambda d=d: me.along(0, d),
            )
            for d in range(1, 4)
        ])
        n_z.append([
            sems.copy(
                lambda u=u, d=d: bzs.at[d, :, columns(u)],
                lambda u=u, d=d: bzr.at[d, :, columns(u)],
                lambda d=d: me.along(2, d),
            )
            for d in range(1, 4)
        ])

    def near_core(u):
        n_core[u].wait()
        cs = columns(u)
        for i in range(2):
            snd[i, :, cs] = (gnf[i, 0:HALF, cs].astype(F32) + cr[i, :, cs].astype(F32)).astype(BF)
        start(n_near[u])
        start(n_y[u])

    def near_y(u):
        wait(n_y[u])
        cs = columns(u)
        sums = []
        for i in range(2):
            t = snd[i, FAR : FAR + 32, cs].astype(F32)
            for d in range(1, 4):
                t = t + yr[d, i, :, cs].astype(F32)
            sums.append(t)
        for d in range(4):
            r = slice(8 * d, 8 * d + 8)
            bxs[d, :, cs] = jnp.concatenate([sums[0][r], sums[1][r]], axis=0).astype(BF)
        start(n_x[u])

    def near_x(u):
        wait(n_x[u])
        cs = columns(u)
        t = bxs[0, :, cs].astype(F32)
        for d in range(1, 4):
            t = t + bxr[d, :, cs].astype(F32)
        for d in range(4):
            bzs[d, 0:2, cs] = t[2 * d : 2 * d + 2]
            bzs[d, 2:4, cs] = t[8 + 2 * d : 10 + 2 * d]
            bzs[d, 4:8, cs] = jnp.zeros((4, t.shape[1]), F32)
        start(n_z[u])

    def near_own(u):
        wait(n_near[u])
        cs = columns(u)
        for i in range(2):
            t = snd[i, 0:32, cs].astype(F32)
            for c in range(1, CHIPS):
                t = t + rr[c, i, :, cs].astype(F32)
            tot[i, :, cs] = t * (1.0 / S1)

    def near_z(u):
        wait(n_z[u])
        cs = columns(u)
        t = bzs[0, :, cs]
        for d in range(1, 4):
            t = t + bzr[d, :, cs]
        t = t * (1.0 / (S1 * S1))
        for i in range(2):
            for r in range(2):
                tot[i, 16 * r : 16 * r + 16, cs] = (
                    tot[i, 16 * r : 16 * r + 16, cs] + t[2 * i + r : 2 * i + r + 1]
                )

        def some(i, carry):
            r = pl.ds(pl.multiple_of(i * S1, S1), S1)
            k_ref[r, cs] = (fine_k[r, cs] + tot[0, pl.ds(i, 1), cs]).astype(BF)
            v_ref[r, cs] = (fine_v[r, cs] + tot[1, pl.ds(i, 1), cs]).astype(BF)
            return carry

        lax.fori_loop(0, ROWS // S1, some, 0, unroll=4)

    pair_row = lax.broadcasted_iota(jnp.int32, (32, ROWS), 0) // S1
    pair_col = lax.broadcasted_iota(jnp.int32, (32, ROWS), 1) // PAIR
    own_pair = pair_row == pair_col

    def forward(h):
        c = pl.ds(pl.multiple_of(h * WIDTH, WIDTH), WIDTH)
        qh = q_ref[:, c]
        s = dot(nf[0, :, c], qh, 1, 1)
        sf = [
            dot(k_ref[p * PAIR : (p + 1) * PAIR, c], qh[p * PAIR : (p + 1) * PAIR], 1, 1)
            for p in range(2)
        ]
        sf = jnp.concatenate(sf, axis=1)
        top = jnp.maximum(jnp.max(s, axis=0, keepdims=True), jnp.max(sf, axis=0, keepdims=True))
        e = jnp.exp2((s - top) * EXP2_SCALE)
        none = jnp.zeros((16, ROWS), F32)
        e = jnp.concatenate(
            [
                jnp.where(own_pair, 0.0, e[0:32]),
                e[32:FAR],
                none,
                e[FAR + 16 : HALF + FAR],
                none,
                e[HALF + FAR + 16 :],
            ],
            axis=0,
        )
        ef = jnp.exp2((sf - top) * EXP2_SCALE)
        total = jnp.sum(e, axis=0, keepdims=True) + jnp.sum(ef, axis=0, keepdims=True)
        e = e.astype(BF)
        ef = ef.astype(BF)
        probs[h, 0:KEYS, :] = e
        probs[h, KEYS : KEYS + PAIR, :] = ef
        out = dot(nf[1, :, c], e, 0, 0)
        of = [
            dot(v_ref[p * PAIR : (p + 1) * PAIR, c], ef[:, p * PAIR : (p + 1) * PAIR], 0, 0)
            for p in range(2)
        ]
        out = out + jnp.concatenate(of, axis=1)
        inv = 1.0 / total
        out = (out * inv).astype(BF)
        att[c, :] = out
        gth = gt[c, :].astype(F32)
        d = jnp.sum(out.astype(F32) * gth, axis=0, keepdims=True) * inv
        delta[h] = jnp.broadcast_to(d, (8, ROWS))
        scaled = gth * inv
        gst[c, :] = scaled.astype(BF)
        gs[:, c] = scaled.T.astype(BF)

    def backward(h):
        c = pl.ds(pl.multiple_of(h * WIDTH, WIDTH), WIDTH)
        qh = q_ref[:, c]
        gth = gst[c, :]
        gh = gs[:, c]
        d = delta[h, 0:1, :]
        e = probs[h, 0:KEYS, :]
        ds = (e.astype(F32) * (dot(nf[1, :, c], gth, 1, 0) - d)).astype(BF)
        gnf[1, :, c] = dot(e, gh, 1, 0).astype(BF)
        gnf[0, :, c] = (dot(ds, qh, 1, 0) * SCALE).astype(BF)
        dq = dot(nf[0, :, c], ds, 0, 0)
        dqf = []
        for p in range(2):
            r = slice(p * PAIR, (p + 1) * PAIR)
            ef = probs[h, KEYS : KEYS + PAIR, r]
            dsf = (ef.astype(F32) * (dot(v_ref[r, c], gth[:, r], 1, 0) - d[:, r])).astype(BF)
            fine_v[r, c] = dot(ef, gh[r], 1, 0)
            fine_k[r, c] = dot(dsf, qh[r], 1, 0) * SCALE
            dqf.append(dot(k_ref[r, c], dsf, 0, 0))
        dq = (dq + jnp.concatenate(dqf, axis=1)) * SCALE
        q_ref[:, c] = dq.T.astype(BF)

    def scheduled(work, plan):
        def step(h, carry):
            work(h)
            for at, actions in plan.items():

                @pl.when(h == at)
                def _():
                    for action, *args in actions:
                        action(*args)

            return carry

        lax.fori_loop(0, HEADS, step, 0)

    def near_send(u):
        n_core[u].start()

    scheduled(
        forward,
        {
            2: [(weigh, 0)],
            3: [(weight_core, 0)],
            5: [(weigh, 1)],
            6: [(weight_core, 1), (weight_a, 0)],
            7: [(weigh, 2), (weight_b, 0)],
        },
    )
    scheduled(
        backward,
        {
            0: [(weight_core, 2), (weight_c, 0), (weight_a, 1)],
            1: [(weight_gather, 0, 2), (weight_b, 1)],
            2: [(near_send, 0), (weight_gather, 0, 1), (weight_a, 2), (weight_c, 1)],
            3: [(near_core, 0), (weight_b, 2), (weight_gather, 1, 2)],
            4: [(weight_gather, 0, 0), (weight_c, 2), (weight_gather, 1, 1)],
            5: [(near_send, 1), (weight_last, 0), (weight_gather, 2, 2)],
            6: [(near_core, 1), (near_y, 0), (weight_gather, 2, 1)],
            7: [(near_send, 2), (near_x, 0), (weight_gather, 1, 0)],
        },
    )
    store_q = pltpu.make_async_copy(q_ref, gq_hbm, store_sem.at[3])
    store_q.start()
    near_core(2)
    near_y(1)
    near_own(0)
    near_z(0)
    weight_last(1)
    near_x(1)
    near_y(2)
    weight_gather(2, 0)
    near_own(1)
    near_z(1)
    near_x(2)
    weight_last(2)
    near_own(2)
    near_z(2)
    store_k = pltpu.make_async_copy(k_ref, gk_hbm, store_sem.at[4])
    store_v = pltpu.make_async_copy(v_ref, gv_hbm, store_sem.at[5])
    store_k.start()
    store_v.start()
    for copy in w_out + [store_q, store_k, store_v]:
        copy.wait()


def finish(
    scale, gq_in, gk_in, gv_in, w_in, gq_out, gk_out, gv_out, w_out, part, wide, in_sem, out_sem
):
    moves = [
        pltpu.make_async_copy(src, dst, in_sem.at[HEADS + i])
        for i, (src, dst) in enumerate(((gq_in, gq_out), (gk_in, gk_out), (gv_in, gv_out)))
    ]
    ins = [pltpu.make_async_copy(w_in.at[h], part.at[h], in_sem.at[h]) for h in range(HEADS)]
    outs = [
        pltpu.make_async_copy(wide.at[h], w_out.at[pl.ds(h * WIDTH, WIDTH)], out_sem.at[h])
        for h in range(HEADS)
    ]
    for copy in ins:
        copy.start()
    for copy in moves:
        copy.start()
    for h in range(HEADS):
        ins[h].wait()
        wide[h] = part[h].astype(F32) * scale
        outs[h].start()
    for copy in outs + moves:
        copy.wait()


def body(queries, key_rows, value_rows, grad_output, out_weight):
    vmem = pltpu.VMEM
    dma = pltpu.SemaphoreType.DMA
    scratch = [
        vmem((ROWS, ALL), BF),
        vmem((ROWS, ALL), BF),
        vmem((ROWS, ALL), BF),
        vmem((ROWS, COLS), BF),
        vmem((ALL, COLS), BF),
        vmem((2, KEYS, ALL), BF),
        vmem((8, ALL // 2), F32),
        vmem((4, 8, ALL // 2), F32),
        vmem((16, ALL), F32),
        vmem((16, ALL), BF),
        vmem((4, 16, ALL), BF),
        vmem((ALL, ROWS), BF),
        vmem((ALL, ROWS), BF),
        vmem((HEADS, KEYS + PAIR, ROWS), BF),
        vmem((ALL, ROWS), BF),
        vmem((ROWS, ALL), BF),
        vmem((HEADS, 8, ROWS), F32),
        vmem((2, KEYS, ALL), BF),
        vmem((2, HALF, ALL), BF),
        vmem((2, HALF, ALL), BF),
        vmem((CHIPS, 2, 32, ALL), BF),
        vmem((4, 2, 32, ALL), BF),
        vmem((4, 16, ALL), BF),
        vmem((4, 16, ALL), BF),
        vmem((4, 8, ALL), F32),
        vmem((4, 8, ALL), F32),
        vmem((ROWS, ALL), F32),
        vmem((ROWS, ALL), F32),
        vmem((2, 32, ALL), F32),
        vmem((HEADS, WIDTH, COLS), BF),
        vmem((HEADS, 64, COLS), BF),
        vmem((3, HEADS, 16, COLS), BF),
        vmem((3, HEADS, 16, 512), BF),
        vmem((3, HEADS, 16, 128), BF),
        vmem((HEADS, 16, COLS), BF),
        vmem((HEADS, 16, 512), BF),
        vmem((HEADS, WIDTH, COLS), BF),
        dma((5,)),
        dma((6,)),
        dma((NSEM,)),
        dma((NSEM,)),
    ]
    hbm = pl.BlockSpec(memory_space=pl.ANY)
    token_shape = jax.ShapeDtypeStruct((ROWS, ALL), BF)
    grads = pl.pallas_call(
        kernel,
        out_shape=(token_shape,) * 3 + (jax.ShapeDtypeStruct((HEADS, WIDTH, COLS), BF),),
        in_specs=[hbm] * 5,
        out_specs=(hbm,) * 4,
        scratch_shapes=scratch,
        compiler_params=pltpu.CompilerParams(
            collective_id=0, has_side_effects=True, vmem_limit_bytes=64 * 1024 * 1024 - 65536
        ),
        name="fused",
    )(queries, key_rows, value_rows, grad_output, out_weight)
    tokens = ROWS * lax.axis_size("node") * lax.axis_size("group")
    return pl.pallas_call(
        functools.partial(finish, 1.0 / math.sqrt(tokens)),
        out_shape=(token_shape,) * 3 + (jax.ShapeDtypeStruct((ALL, COLS), F32),),
        in_specs=[hbm] * 4,
        out_specs=(hbm,) * 4,
        scratch_shapes=[
            vmem((HEADS, WIDTH, COLS), BF),
            vmem((HEADS, WIDTH, COLS), F32),
            dma((HEADS + 3,)),
            dma((HEADS,)),
        ],
        compiler_params=pltpu.CompilerParams(vmem_limit_bytes=32 * 1024 * 1024),
        name="finish",
    )(*grads)


def solution(mesh):
    split = P(("group", "node"), None)
    return jax.shard_map(
        body,
        mesh=mesh,
        in_specs=(split, split, split, split, P()),
        out_specs=(split, split, split, P()),
        check_vma=False,
    )
```

```python
import functools
import math

import jax
import jax.numpy as jnp
from jax import lax
from jax.experimental import pallas as pl
from jax.experimental.pallas import tpu as pltpu
from jax.sharding import PartitionSpec as P

HEADS = 8
WIDTH = 128
S1 = 16
ROWS = 512
PAIR = 256
CHIPS = 8
KEYS = 768
HALF = 384
FAR = 256
COLS = 2048
ALL = HEADS * WIDTH
UNITS = ((0, 3), (3, 3), (6, 2))
ORDERS = (
    (1, 0, 2), (0, 1, 2), (2, 0, 1), (1, 0, 2), (0, 1, 2), (2, 1, 0), (1, 2, 0), (0, 2, 1),
)
NSEM = 232
BF = jnp.bfloat16
F32 = jnp.float32
SCALE = 1.0 / math.sqrt(WIDTH)
EXP2_SCALE = math.log2(math.e) / math.sqrt(WIDTH)


def dot(a, b, ca, cb):
    return lax.dot_general(a, b, (((ca,), (cb,)), ((), ())), preferred_element_type=F32)


def flip4(a, d):
    if d == 0:
        return a
    if d == 1:
        return a + 1 - 2 * (a % 2)
    if d == 2:
        return (a + 2) % 4
    return 3 - a


def flip2(a, d):
    return 1 - a if d else a


class Place:
    def __init__(self):
        node = lax.axis_index("node")
        group = lax.axis_index("group")
        self.core = node % 2
        z = (node // 2) % 4
        x_lo = node // 8
        x_hi = group // 4
        y = group % 4
        los, his = [flip2(x_lo, d) for d in range(2)], [flip2(x_hi, d) for d in range(2)]
        zs, ys = [flip4(z, d) for d in range(4)], [flip4(y, d) for d in range(4)]
        self.flips = [[his[d // 2] * 2 + los[d % 2] for d in range(4)], ys, zs]
        self.sib = {"node": node + 1 - 2 * self.core, "group": group}
        self.crosses = [
            {"node": (los[m // 4 % 2] * 4 + zs[m % 4]) * 2 + self.core, "group": his[m // 8] * 4 + y}
            for m in range(16)
        ]
        self.ys = [{"node": node, "group": x_hi * 4 + ys[d]} for d in range(4)]

    def coord_flip(self, axis, d):
        return self.flips[axis][d]

    def sibling(self):
        return self.sib

    def cross(self, m):
        return self.crosses[m]

    def chip(self, c):
        return self.crosses[c]

    def along(self, axis, d):
        return (self.crosses[4 * d], self.ys[d], self.crosses[d])[axis]


class Sems:
    def __init__(self, send_sems, recv_sems):
        self.send_sems, self.recv_sems, self.used = send_sems, recv_sems, 0

    def copy(self, src, dst, device):
        i = self.used
        self.used += 1
        return Copy(src, dst, self.send_sems.at[i], self.recv_sems.at[i], device)


class Copy:
    def __init__(self, src, dst, send_sem, recv_sem, device):
        self.parts = src, dst, send_sem, recv_sem, device

    def make(self):
        src, dst, send_sem, recv_sem, device = self.parts
        return pltpu.make_async_remote_copy(
            src_ref=src(),
            dst_ref=dst(),
            send_sem=send_sem,
            recv_sem=recv_sem,
            device_id=device(),
            device_id_type=pl.DeviceIdType.MESH,
        )

    def start(self):
        self.make().start()

    def wait(self):
        self.make().wait()


def start(copies):
    for copy in copies:
        copy.start()


def wait(copies):
    for copy in copies:
        copy.wait()


def kernel(
    q_hbm, k_hbm, v_hbm, go_hbm, w_hbm,
    gq_hbm, gk_hbm, gv_hbm, wout_hbm,
    q_ref, k_ref, v_ref, go_ref, w_ref,
    nf, zsend, zrecv, xblk, gt, att, probs, gst, gs, delta,
    gnf, cr, near_snd, far_snd, zr, xs, xr, yr, packed, bxs, bxr, fine_k, fine_v, tot,
    wpart, wr0, ra, rb, rc, sa, sb, wout,
    load_sem, store_sem, send_sems, recv_sems,
):
    me = Place()
    core = me.core
    sems = Sems(send_sems, recv_sems)

    barrier = pltpu.get_barrier_semaphore()
    partners = [me.sibling()]
    partners += [me.cross(m) for m in range(1, 16)]
    partners += [me.along(1, d) for d in range(1, 4)]
    for partner in partners:
        pl.semaphore_signal(barrier, inc=1, device_id=partner, device_id_type=pl.DeviceIdType.MESH)

    loads = [
        pltpu.make_async_copy(src, dst, load_sem.at[i])
        for i, (src, dst) in enumerate(
            ((k_hbm, k_ref), (v_hbm, v_ref), (go_hbm, go_ref), (w_hbm, w_ref), (q_hbm, q_ref))
        )
    ]
    for load in loads:
        load.start()

    def near_at(c):
        return lambda: nf.at[:, pl.ds(32 * c, 32), :]

    def far_at(d):
        return lambda: nf.at[:, pl.ds(FAR + 32 * d, 32), :]

    def sib_at(first, rows):
        return lambda: nf.at[:, pl.ds(HALF + first, rows), :]

    own_gather = [
        sems.copy(lambda: zsend, lambda m=m: zrecv.at[m], lambda m=m: me.cross(m))
        for m in range(1, 16)
    ]
    y_gather = [
        sems.copy(far_at(0), far_at(d), lambda d=d: me.along(1, d)) for d in range(1, 4)
    ]
    near_gather = [
        sems.copy(near_at(0), near_at(c), lambda c=c: me.chip(c)) for c in range(1, CHIPS)
    ]
    near_forward = [
        sems.copy(near_at(c), sib_at(32 * c, 32), me.sibling) for c in range(CHIPS)
    ]
    far_forward = [
        sems.copy(far_at(d), sib_at(FAR + 32 * d, 32), me.sibling) for d in range(4)
    ]

    rows = lax.broadcasted_iota(jnp.int32, (32, ROWS), 0)
    toks = lax.broadcasted_iota(jnp.int32, (32, ROWS), 1)
    mean16 = jnp.where(toks // S1 == rows, 1.0 / S1, 0.0).astype(BF)
    r8 = lax.broadcasted_iota(jnp.int32, (8, 32), 0)
    c8 = lax.broadcasted_iota(jnp.int32, (8, 32), 1) // 16
    pick_k = jnp.where(c8 == r8, 1.0 / S1, 0.0).astype(BF)
    pick_v = jnp.where(c8 + 2 == r8, 1.0 / S1, 0.0).astype(BF)
    loads[0].wait()
    near_k = dot(mean16, k_ref[...], 1, 0).astype(BF)
    nf[0, 0:32, :] = near_k
    loads[1].wait()
    near_v = dot(mean16, v_ref[...], 1, 0).astype(BF)
    nf[1, 0:32, :] = near_v
    far_own = (dot(pick_k, near_k, 1, 0) + dot(pick_v, near_v, 1, 0)).astype(BF).astype(F32)
    zsend[...] = jnp.concatenate(
        [far_own[0:4, 256 * part : 256 * part + 256] for part in range(4)], axis=0
    ).astype(BF)

    pl.semaphore_wait(barrier, len(partners))
    start(own_gather)
    start(near_gather)
    near_forward[0].start()

    def project(i, carry):
        r = pl.ds(pl.multiple_of(i * 256, 256), 256)
        gt[r, :] = dot(w_ref[r, :], go_ref[...], 1, 1).astype(BF)
        return carry

    loads[2].wait()
    loads[3].wait()
    lax.fori_loop(0, 4, project, 0)

    wait(own_gather)
    for m in range(16):
        block = (zsend[...] if m == 0 else zrecv[m]).astype(F32)
        for i in range(2):
            for part in range(4):
                xblk[i, 2 * m : 2 * m + 2, part * 256 : part * 256 + 256] = block[
                    4 * part + 2 * i : 4 * part + 2 * i + 2
                ]
    nf[:, FAR : FAR + 32, :] = xblk[...].astype(BF)
    start(y_gather)
    far_forward[0].start()
    loads[4].wait()
    for c in range(1, CHIPS):
        near_gather[c - 1].wait()
        near_forward[c].start()
    for d in range(1, 4):
        y_gather[d - 1].wait()
        far_forward[d].start()
    wait(near_forward)
    wait(far_forward)

    mine = pl.multiple_of(core * 64, 64)
    other = pl.multiple_of((1 - core) * 64, 64)

    def heads(u):
        return range(UNITS[u][0], UNITS[u][0] + UNITS[u][1])

    def span(u):
        return pl.ds(*UNITS[u])

    def columns(u):
        return pl.ds(UNITS[u][0] * WIDTH, UNITS[u][1] * WIDTH)

    def offsets(unit, first=0):
        return [
            [pl.multiple_of(first + me.coord_flip(axis, d) * unit, unit) for d in range(4)]
            for axis in range(3)
        ]

    rows_a, cols_b, cols_c = offsets(16, mine), offsets(512), offsets(128)
    cols_bc = [
        [pl.multiple_of(cols_b[b][0] + cols_c[c][0], 128) for c in range(3)] for b in range(3)
    ]

    def row_a(h, d=0):
        return rows_a[ORDERS[h][0]][d]

    def col_b(h, d=0):
        return cols_b[ORDERS[h][1]][d]

    def col_c(h, d=0):
        return cols_c[ORDERS[h][2]][d]

    def col_bc(h):
        return cols_bc[ORDERS[h][1]][ORDERS[h][2]]

    def piece(h, step):
        if step == 2:
            return wout.at[h, pl.ds(row_a(h), 16), pl.ds(col_bc(h), 128)]
        if step == 1:
            return wout.at[h, pl.ds(row_a(h), 16), pl.ds(col_b(h), 512)]
        return wout.at[h, pl.ds(row_a(h), 16), :]

    w_core, w_a, w_b, w_c, w_g, w_sib, w_out = [], [], [], [], [[], [], []], [], []
    for u in range(3):
        w_core.append(
            sems.copy(
                lambda u=u: wpart.at[span(u), pl.ds(other, 64), :],
                lambda u=u: wr0.at[span(u)],
                me.sibling,
            )
        )
        w_sib.append(
            sems.copy(
                lambda u=u: wout.at[span(u), pl.ds(mine, 64), :],
                lambda u=u: wout.at[span(u), pl.ds(mine, 64), :],
                me.sibling,
            )
        )
        w_out.append(
            pltpu.make_async_copy(wout.at[span(u)], wout_hbm.at[span(u)], store_sem.at[u])
        )
        w_a.append([
            sems.copy(
                lambda h=h, d=d: wpart.at[h, pl.ds(row_a(h, d), 16), :],
                lambda h=h, d=d: ra.at[d - 1, h],
                lambda h=h, d=d: me.along(ORDERS[h][0], d),
            )
            for h in heads(u) for d in range(1, 4)
        ])
        w_b.append([
            sems.copy(
                lambda h=h, d=d: sa.at[h, :, pl.ds(col_b(h, d), 512)],
                lambda h=h, d=d: rb.at[d - 1, h],
                lambda h=h, d=d: me.along(ORDERS[h][1], d),
            )
            for h in heads(u) for d in range(1, 4)
        ])
        w_c.append([
            sems.copy(
                lambda h=h, d=d: sb.at[h, :, pl.ds(col_c(h, d), 128)],
                lambda h=h, d=d: rc.at[d - 1, h],
                lambda h=h, d=d: me.along(ORDERS[h][2], d),
            )
            for h in heads(u) for d in range(1, 4)
        ])
        for step in range(3):
            w_g[step].append([
                sems.copy(
                    lambda h=h, step=step: piece(h, step),
                    lambda h=h, step=step: piece(h, step),
                    lambda h=h, d=d, step=step: me.along(ORDERS[h][step], d),
                )
                for h in heads(u) for d in range(1, 4)
            ])

    def weigh(u):
        def some(i, carry):
            c = pl.ds(pl.multiple_of(i * 512, 512), 512)
            part = dot(att[columns(u), :], go_ref[:, c], 1, 0)
            wpart[span(u), :, c] = part.reshape(UNITS[u][1], WIDTH, 512).astype(BF)
            return carry

        lax.fori_loop(0, COLS // 512, some, 0)
        w_core[u].start()

    def weight_core(u):
        w_core[u].wait()

        def some(h, carry):
            r = pl.ds(mine, 64)
            wpart[h, r, :] = (wpart[h, r, :].astype(F32) + wr0[h].astype(F32)).astype(BF)
            return carry

        lax.fori_loop(heads(u)[0], heads(u)[-1] + 1, some, 0)
        start(w_a[u])

    def weight_a(u):
        wait(w_a[u])
        for h in heads(u):
            t = wpart[h, pl.ds(row_a(h), 16), :].astype(F32)
            for d in range(3):
                t = t + ra[d, h].astype(F32)
            sa[h] = t.astype(BF)
        start(w_b[u])

    def weight_b(u):
        wait(w_b[u])
        for h in heads(u):
            t = sa[h, :, pl.ds(col_b(h), 512)].astype(F32)
            for d in range(3):
                t = t + rb[d, h].astype(F32)
            sb[h] = t.astype(BF)
        start(w_c[u])

    def weight_c(u):
        wait(w_c[u])
        for h in heads(u):
            t = sb[h, :, pl.ds(col_c(h), 128)].astype(F32)
            for d in range(3):
                t = t + rc[d, h].astype(F32)
            wout[h, pl.ds(row_a(h), 16), pl.ds(col_bc(h), 128)] = t.astype(BF)
        start(w_g[2][u])

    def weight_gather(u, step):
        wait(w_g[step][u])
        if step > 0:
            start(w_g[step - 1][u])
        else:
            w_sib[u].start()

    def weight_last(u):
        w_sib[u].wait()
        w_out[u].start()

    n_core, n_z, n_x, n_y = [], [], [], []
    for u in range(3):
        n_core.append(
            sems.copy(
                lambda u=u: gnf.at[:, pl.ds(HALF, HALF), columns(u)],
                lambda u=u: cr.at[:, :, columns(u)],
                me.sibling,
            )
        )
        n_z.append([
            sems.copy(
                lambda u=u, d=d: near_snd.at[:, :, d, :, columns(u)],
                lambda u=u, d=d: zr.at[d, :, :, :, columns(u)],
                lambda d=d: me.along(2, d),
            )
            for d in range(1, 4)
        ])
        n_x.append(
            sems.copy(
                lambda u=u: xs.at[:, :, columns(u)],
                lambda u=u: xr.at[:, :, columns(u)],
                lambda: me.chip(4),
            )
        )
        n_y.append([
            sems.copy(
                lambda u=u, d=d: far_snd.at[:, pl.ds(32 * d, 32), columns(u)],
                lambda u=u, d=d: yr.at[d, :, :, columns(u)],
                lambda d=d: me.along(1, d),
            )
            for d in range(1, 4)
        ])
    own_reduce = [
        sems.copy(lambda m=m: bxs.at[m], lambda m=m: bxr.at[m], lambda m=m: me.cross(m))
        for m in range(1, 16)
    ]

    def near_core(u):
        n_core[u].wait()
        cs = columns(u)
        for i in range(2):
            t = (gnf[i, 0:HALF, cs].astype(F32) + cr[i, :, cs].astype(F32)).astype(BF)
            for c in range(CHIPS):
                near_snd[i, c // 4, c % 4, :, cs] = t[32 * c : 32 * c + 32]
            far_snd[i, :, cs] = t[FAR:]
        start(n_z[u])
        start(n_y[u])

    def near_z(u):
        wait(n_z[u])
        cs = columns(u)
        for i in range(2):
            for x in range(2):
                t = near_snd[i, x, 0, :, cs].astype(F32)
                for d in range(1, 4):
                    t = t + zr[d, i, x, :, cs].astype(F32)
                if x == 0:
                    tot[i, :, cs] = t
                else:
                    xs[i, :, cs] = t.astype(BF)
        n_x[u].start()

    def near_x(u):
        n_x[u].wait()
        cs = columns(u)
        for i in range(2):
            tot[i, :, cs] = (tot[i, :, cs] + xr[i, :, cs].astype(F32)) * (1.0 / S1)

    def near_y(u):
        wait(n_y[u])
        cs = columns(u)
        for i in range(2):
            t = far_snd[i, 0:32, cs].astype(F32)
            for d in range(1, 4):
                t = t + yr[d, i, :, cs].astype(F32)
            xblk[i, :, cs] = t
        for part in ((), (0, 1, 2), (3,))[u]:
            for m in range(16):
                for i in range(2):
                    packed[m, 4 * part + 2 * i : 4 * part + 2 * i + 2, :] = xblk[
                        i, 2 * m : 2 * m + 2, part * 256 : part * 256 + 256
                    ]
        if u == 2:
            bxs[...] = packed[...].astype(BF)
            start(own_reduce)

    def finish_rows():
        wait(own_reduce)
        t = bxs[0].astype(F32)
        for m in range(1, 16):
            t = t + bxr[m].astype(F32)
        t = t * (1.0 / (S1 * S1))
        for i in range(2):
            for r in range(2):
                far_row = jnp.concatenate(
                    [t[4 * p + 2 * i + r : 4 * p + 2 * i + r + 1] for p in range(4)], axis=1
                )
                tot[i, 16 * r : 16 * r + 16, :] = tot[i, 16 * r : 16 * r + 16, :] + far_row

        def some(i, carry):
            r = pl.ds(pl.multiple_of(i * S1, S1), S1)
            k_ref[r, :] = (fine_k[r, :] + tot[0, pl.ds(i, 1), :]).astype(BF)
            v_ref[r, :] = (fine_v[r, :] + tot[1, pl.ds(i, 1), :]).astype(BF)
            return carry

        lax.fori_loop(0, ROWS // S1, some, 0, unroll=2)

    pair_row = lax.broadcasted_iota(jnp.int32, (32, ROWS), 0) // S1
    pair_col = lax.broadcasted_iota(jnp.int32, (32, ROWS), 1) // PAIR
    own_pair = pair_row == pair_col

    def forward(h):
        c = pl.ds(pl.multiple_of(h * WIDTH, WIDTH), WIDTH)
        qh = q_ref[:, c]
        s = dot(nf[0, :, c], qh, 1, 1)
        sf = [
            dot(k_ref[p * PAIR : (p + 1) * PAIR, c], qh[p * PAIR : (p + 1) * PAIR], 1, 1)
            for p in range(2)
        ]
        sf = jnp.concatenate(sf, axis=1)
        top = jnp.maximum(jnp.max(s, axis=0, keepdims=True), jnp.max(sf, axis=0, keepdims=True))
        e = jnp.exp2((s - top) * EXP2_SCALE)
        none = jnp.zeros((16, ROWS), F32)
        e = jnp.concatenate(
            [
                jnp.where(own_pair, 0.0, e[0:32]),
                e[32:FAR],
                none,
                e[FAR + 16 : HALF + FAR],
                none,
                e[HALF + FAR + 16 :],
            ],
            axis=0,
        )
        ef = jnp.exp2((sf - top) * EXP2_SCALE)
        total = jnp.sum(e, axis=0, keepdims=True) + jnp.sum(ef, axis=0, keepdims=True)
        e = e.astype(BF)
        ef = ef.astype(BF)
        probs[h, 0:KEYS, :] = e
        probs[h, KEYS : KEYS + PAIR, :] = ef
        out = dot(nf[1, :, c], e, 0, 0)
        of = [
            dot(v_ref[p * PAIR : (p + 1) * PAIR, c], ef[:, p * PAIR : (p + 1) * PAIR], 0, 0)
            for p in range(2)
        ]
        out = out + jnp.concatenate(of, axis=1)
        inv = 1.0 / total
        out = (out * inv).astype(BF)
        att[c, :] = out
        gth = gt[c, :].astype(F32)
        d = jnp.sum(out.astype(F32) * gth, axis=0, keepdims=True) * inv
        delta[h] = jnp.broadcast_to(d, (8, ROWS))
        scaled = gth * inv
        gst[c, :] = scaled.astype(BF)
        gs[:, c] = scaled.T.astype(BF)

    def backward(h):
        c = pl.ds(pl.multiple_of(h * WIDTH, WIDTH), WIDTH)
        qh = q_ref[:, c]
        gth = gst[c, :]
        gh = gs[:, c]
        d = delta[h, 0:1, :]
        e = probs[h, 0:KEYS, :]
        ds = (e.astype(F32) * (dot(nf[1, :, c], gth, 1, 0) - d)).astype(BF)
        gnf[1, :, c] = dot(e, gh, 1, 0).astype(BF)
        gnf[0, :, c] = (dot(ds, qh, 1, 0) * SCALE).astype(BF)
        dq = dot(nf[0, :, c], ds, 0, 0)
        dqf = []
        for p in range(2):
            r = slice(p * PAIR, (p + 1) * PAIR)
            ef = probs[h, KEYS : KEYS + PAIR, r]
            dsf = (ef.astype(F32) * (dot(v_ref[r, c], gth[:, r], 1, 0) - d[:, r])).astype(BF)
            fine_v[r, c] = dot(ef, gh[r], 1, 0)
            fine_k[r, c] = dot(dsf, qh[r], 1, 0) * SCALE
            dqf.append(dot(k_ref[r, c], dsf, 0, 0))
        dq = (dq + jnp.concatenate(dqf, axis=1)) * SCALE
        q_ref[:, c] = dq.T.astype(BF)

    def scheduled(work, plan):
        def step(h, carry):
            work(h)
            for at, actions in plan.items():

                @pl.when(h == at)
                def _():
                    for action, *args in actions:
                        action(*args)

            return carry

        lax.fori_loop(0, HEADS, step, 0)

    def near_send(u):
        n_core[u].start()

    scheduled(
        forward,
        {
            2: [(weigh, 0)],
            3: [(weight_core, 0)],
            5: [(weigh, 1)],
            6: [(weight_core, 1)],
            7: [(weight_a, 0), (weigh, 2)],
        },
    )
    scheduled(
        backward,
        {
            0: [(weight_core, 2)],
            1: [(weight_a, 1)],
            2: [(near_send, 0), (weight_b, 0)],
            3: [(near_core, 0)],
            4: [(weight_a, 2), (weight_b, 1)],
            5: [(near_send, 1), (weight_c, 0)],
            6: [(near_core, 1), (weight_c, 1)],
            7: [(near_send, 2), (weight_b, 2), (weight_gather, 0, 2), (near_z, 0)],
        },
    )
    store_q = pltpu.make_async_copy(q_ref, gq_hbm, store_sem.at[3])
    store_q.start()
    near_core(2)
    weight_gather(1, 2)
    near_y(0)
    weight_c(2)
    weight_gather(0, 1)
    near_z(1)
    near_y(1)
    weight_gather(1, 1)
    near_y(2)
    weight_gather(2, 2)
    near_z(2)
    weight_gather(0, 0)
    weight_gather(1, 0)
    near_x(0)
    near_x(1)
    weight_gather(2, 1)
    weight_last(0)
    weight_last(1)
    near_x(2)
    finish_rows()
    store_k = pltpu.make_async_copy(k_ref, gk_hbm, store_sem.at[4])
    store_v = pltpu.make_async_copy(v_ref, gv_hbm, store_sem.at[5])
    store_k.start()
    store_v.start()
    weight_gather(2, 0)
    weight_last(2)
    for copy in w_out + [store_q, store_k, store_v]:
        copy.wait()


def finish(
    scale, gq_in, gk_in, gv_in, w_in, gq_out, gk_out, gv_out, w_out,
    part, wide, kept, in_sem, out_sem,
):
    ins = [pltpu.make_async_copy(w_in.at[h], part.at[h], in_sem.at[h]) for h in range(HEADS)]
    outs = [
        pltpu.make_async_copy(wide.at[h], w_out.at[pl.ds(h * WIDTH, WIDTH)], out_sem.at[h])
        for h in range(HEADS)
    ]
    for i, (src, dst) in enumerate(((gq_in, gq_out), (gk_in, gk_out), (gv_in, gv_out))):
        ins.append(pltpu.make_async_copy(src, kept.at[i], in_sem.at[HEADS + i]))
        outs.append(pltpu.make_async_copy(kept.at[i], dst, out_sem.at[HEADS + i]))
    for copy in ins:
        copy.start()
    for h in range(HEADS):
        ins[h].wait()
        wide[h] = part[h].astype(F32) * scale
        outs[h].start()
    for i in range(HEADS, HEADS + 3):
        ins[i].wait()
        outs[i].start()
    for copy in outs:
        copy.wait()


def body(queries, key_rows, value_rows, grad_output, out_weight):
    vmem = pltpu.VMEM
    dma = pltpu.SemaphoreType.DMA
    scratch = [
        vmem((ROWS, ALL), BF),
        vmem((ROWS, ALL), BF),
        vmem((ROWS, ALL), BF),
        vmem((ROWS, COLS), BF),
        vmem((ALL, COLS), BF),
        vmem((2, KEYS, ALL), BF),
        vmem((16, 256), BF),
        vmem((16, 16, 256), BF),
        vmem((2, 32, ALL), F32),
        vmem((ALL, ROWS), BF),
        vmem((ALL, ROWS), BF),
        vmem((HEADS, KEYS + PAIR, ROWS), BF),
        vmem((ALL, ROWS), BF),
        vmem((ROWS, ALL), BF),
        vmem((HEADS, 8, ROWS), F32),
        vmem((2, KEYS, ALL), BF),
        vmem((2, HALF, ALL), BF),
        vmem((2, 2, 4, 32, ALL), BF),
        vmem((2, 128, ALL), BF),
        vmem((4, 2, 2, 32, ALL), BF),
        vmem((2, 32, ALL), BF),
        vmem((2, 32, ALL), BF),
        vmem((4, 2, 32, ALL), BF),
        vmem((16, 16, 256), F32),
        vmem((16, 16, 256), BF),
        vmem((16, 16, 256), BF),
        vmem((ROWS, ALL), F32),
        vmem((ROWS, ALL), F32),
        vmem((2, 32, ALL), F32),
        vmem((HEADS, WIDTH, COLS), BF),
        vmem((HEADS, 64, COLS), BF),
        vmem((3, HEADS, 16, COLS), BF),
        vmem((3, HEADS, 16, 512), BF),
        vmem((3, HEADS, 16, 128), BF),
        vmem((HEADS, 16, COLS), BF),
        vmem((HEADS, 16, 512), BF),
        vmem((HEADS, WIDTH, COLS), BF),
        dma((5,)),
        dma((6,)),
        dma((NSEM,)),
        dma((NSEM,)),
    ]
    hbm = pl.BlockSpec(memory_space=pl.ANY)
    token_shape = jax.ShapeDtypeStruct((ROWS, ALL), BF)
    grads = pl.pallas_call(
        kernel,
        out_shape=(token_shape,) * 3 + (jax.ShapeDtypeStruct((HEADS, WIDTH, COLS), BF),),
        in_specs=[hbm] * 5,
        out_specs=(hbm,) * 4,
        scratch_shapes=scratch,
        compiler_params=pltpu.CompilerParams(
            collective_id=0, has_side_effects=True, vmem_limit_bytes=64 * 1024 * 1024 - 65536
        ),
        name="fused",
    )(queries, key_rows, value_rows, grad_output, out_weight)
    tokens = ROWS * lax.axis_size("node") * lax.axis_size("group")
    return pl.pallas_call(
        functools.partial(finish, 1.0 / math.sqrt(tokens)),
        out_shape=(token_shape,) * 3 + (jax.ShapeDtypeStruct((ALL, COLS), F32),),
        in_specs=[hbm] * 4,
        out_specs=(hbm,) * 4,
        scratch_shapes=[
            vmem((HEADS, WIDTH, COLS), BF),
            vmem((HEADS, WIDTH, COLS), F32),
            vmem((3, ROWS, ALL), BF),
            dma((HEADS + 3,)),
            dma((HEADS + 3,)),
        ],
        compiler_params=pltpu.CompilerParams(vmem_limit_bytes=64 * 1024 * 1024 - 65536),
        name="finish",
    )(*grads)


def solution(mesh):
    split = P(("group", "node"), None)
    return jax.shard_map(
        body,
        mesh=mesh,
        in_specs=(split, split, split, split, P()),
        out_specs=(split, split, split, P()),
        check_vma=False,
    )
```

```python
import functools
import math

import jax
import jax.numpy as jnp
from jax import lax
from jax.experimental import pallas as pl
from jax.experimental.pallas import tpu as pltpu
from jax.sharding import PartitionSpec as P

HEADS = 8
WIDTH = 128
S1 = 16
ROWS = 512
PAIR = 256
CHIPS = 8
KEYS = 768
HALF = 384
FAR = 256
COLS = 2048
ALL = HEADS * WIDTH
UNITS = ((0, 3), (3, 3), (6, 2))
ORDERS = (
    (1, 0, 2), (0, 1, 2), (2, 0, 1), (1, 0, 2), (0, 1, 2), (2, 1, 0), (1, 2, 0), (0, 2, 1),
)
NSEM = 280
BF = jnp.bfloat16
F32 = jnp.float32
SCALE = 1.0 / math.sqrt(WIDTH)
EXP2_SCALE = math.log2(math.e) / math.sqrt(WIDTH)


def dot(a, b, ca, cb):
    return lax.dot_general(a, b, (((ca,), (cb,)), ((), ())), preferred_element_type=F32)


def flip4(a, d):
    if d == 0:
        return a
    if d == 1:
        return a + 1 - 2 * (a % 2)
    if d == 2:
        return (a + 2) % 4
    return 3 - a


def flip2(a, d):
    return 1 - a if d else a


class Place:
    def __init__(self):
        node = lax.axis_index("node")
        group = lax.axis_index("group")
        self.core = node % 2
        z = (node // 2) % 4
        x_lo = node // 8
        x_hi = group // 4
        y = group % 4
        los, his = [flip2(x_lo, d) for d in range(2)], [flip2(x_hi, d) for d in range(2)]
        zs, ys = [flip4(z, d) for d in range(4)], [flip4(y, d) for d in range(4)]
        self.flips = [[his[d // 2] * 2 + los[d % 2] for d in range(4)], ys, zs]
        self.sib = {"node": node + 1 - 2 * self.core, "group": group}
        self.crosses = [
            {"node": (los[m // 4 % 2] * 4 + zs[m % 4]) * 2 + self.core, "group": his[m // 8] * 4 + y}
            for m in range(16)
        ]
        self.ys = [{"node": node, "group": x_hi * 4 + ys[d]} for d in range(4)]

    def coord_flip(self, axis, d):
        return self.flips[axis][d]

    def sibling(self):
        return self.sib

    def cross(self, m):
        return self.crosses[m]

    def chip(self, c):
        return self.crosses[c]

    def along(self, axis, d):
        return (self.crosses[4 * d], self.ys[d], self.crosses[d])[axis]


class Sems:
    def __init__(self, send_sems, recv_sems):
        self.send_sems, self.recv_sems, self.used = send_sems, recv_sems, 0

    def copy(self, src, dst, device):
        i = self.used
        self.used += 1
        return Copy(src, dst, self.send_sems.at[i], self.recv_sems.at[i], device)


class Copy:
    def __init__(self, src, dst, send_sem, recv_sem, device):
        self.parts = src, dst, send_sem, recv_sem, device

    def make(self):
        src, dst, send_sem, recv_sem, device = self.parts
        return pltpu.make_async_remote_copy(
            src_ref=src(),
            dst_ref=dst(),
            send_sem=send_sem,
            recv_sem=recv_sem,
            device_id=device(),
            device_id_type=pl.DeviceIdType.MESH,
        )

    def start(self):
        self.make().start()

    def wait(self):
        self.make().wait()


def start(copies):
    for copy in copies:
        copy.start()


def wait(copies):
    for copy in copies:
        copy.wait()


def kernel(
    q_hbm, k_hbm, v_hbm, go_hbm, w_hbm,
    gq_hbm, gk_hbm, gv_hbm, wout_hbm,
    q_ref, k_ref, v_ref, go_ref, w_ref,
    nf, zsend, zrecv, xblk, gt, att, probs, gst, gs, delta,
    gnf, cr, near_snd, far_snd, zr, xs, xr, yr, packed, bxs, bxr, fine_k, fine_v, tot,
    wpart, wr0, ra, rb, rc, sa, sb, wout,
    load_sem, store_sem, send_sems, recv_sems,
):
    me = Place()
    core = me.core
    sems = Sems(send_sems, recv_sems)

    barrier = pltpu.get_barrier_semaphore()
    partners = [me.sibling()]
    partners += [me.cross(m) for m in range(1, 16)]
    partners += [me.along(1, d) for d in range(1, 4)]
    for partner in partners:
        pl.semaphore_signal(barrier, inc=1, device_id=partner, device_id_type=pl.DeviceIdType.MESH)

    loads = [
        pltpu.make_async_copy(src, dst, load_sem.at[i])
        for i, (src, dst) in enumerate(
            ((k_hbm, k_ref), (v_hbm, v_ref), (go_hbm, go_ref), (w_hbm, w_ref), (q_hbm, q_ref))
        )
    ]
    for load in loads:
        load.start()

    def heads(u):
        return range(UNITS[u][0], UNITS[u][0] + UNITS[u][1])

    def span(u):
        return pl.ds(*UNITS[u])

    def columns(u):
        return pl.ds(UNITS[u][0] * WIDTH, UNITS[u][1] * WIDTH)

    def near_at(c, u):
        return lambda: nf.at[:, pl.ds(32 * c, 32), columns(u)]

    def far_at(d, u):
        return lambda: nf.at[:, pl.ds(FAR + 32 * d, 32), columns(u)]

    def sib_at(first, u):
        return lambda: nf.at[:, pl.ds(HALF + first, 32), columns(u)]

    own_gather = [
        sems.copy(lambda: zsend, lambda m=m: zrecv.at[m], lambda m=m: me.cross(m))
        for m in range(1, 16)
    ]
    y_gather = [
        [sems.copy(far_at(0, u), far_at(d, u), lambda d=d: me.along(1, d)) for d in range(1, 4)]
        for u in range(3)
    ]
    near_gather = [
        [sems.copy(near_at(0, u), near_at(c, u), lambda c=c: me.chip(c)) for c in range(1, CHIPS)]
        for u in range(3)
    ]
    near_forward = [
        [sems.copy(near_at(c, u), sib_at(32 * c, u), me.sibling) for c in range(CHIPS)]
        for u in range(3)
    ]
    far_forward = [
        [sems.copy(far_at(d, u), sib_at(FAR + 32 * d, u), me.sibling) for d in range(4)]
        for u in range(3)
    ]

    rows = lax.broadcasted_iota(jnp.int32, (32, ROWS), 0)
    toks = lax.broadcasted_iota(jnp.int32, (32, ROWS), 1)
    mean16 = jnp.where(toks // S1 == rows, 1.0 / S1, 0.0).astype(BF)
    r8 = lax.broadcasted_iota(jnp.int32, (8, 32), 0)
    c8 = lax.broadcasted_iota(jnp.int32, (8, 32), 1) // 16
    pick_k = jnp.where(c8 == r8, 1.0 / S1, 0.0).astype(BF)
    pick_v = jnp.where(c8 + 2 == r8, 1.0 / S1, 0.0).astype(BF)
    loads[0].wait()
    near_k = dot(mean16, k_ref[...], 1, 0).astype(BF)
    nf[0, 0:32, :] = near_k
    loads[1].wait()
    near_v = dot(mean16, v_ref[...], 1, 0).astype(BF)
    nf[1, 0:32, :] = near_v
    far_own = (dot(pick_k, near_k, 1, 0) + dot(pick_v, near_v, 1, 0)).astype(BF).astype(F32)
    zsend[...] = jnp.concatenate(
        [far_own[0:4, 256 * part : 256 * part + 256] for part in range(4)], axis=0
    ).astype(BF)

    pl.semaphore_wait(barrier, len(partners))
    start(own_gather)
    for u in range(3):
        start(near_gather[u])
        near_forward[u][0].start()

    def project(i, carry):
        r = pl.ds(pl.multiple_of(i * 256, 256), 256)
        gt[r, :] = dot(w_ref[r, :], go_ref[...], 1, 1).astype(BF)
        return carry

    loads[2].wait()
    loads[3].wait()
    lax.fori_loop(0, 4, project, 0)

    wait(own_gather)
    for m in range(16):
        block = (zsend[...] if m == 0 else zrecv[m]).astype(F32)
        for i in range(2):
            for part in range(4):
                xblk[i, 2 * m : 2 * m + 2, part * 256 : part * 256 + 256] = block[
                    4 * part + 2 * i : 4 * part + 2 * i + 2
                ]
    nf[:, FAR : FAR + 32, :] = xblk[...].astype(BF)
    for u in range(3):
        start(y_gather[u])
        far_forward[u][0].start()
    loads[4].wait()

    def gather_near(u):
        for c in range(1, CHIPS):
            near_gather[u][c - 1].wait()
            near_forward[u][c].start()

    def gather_far(u):
        for d in range(1, 4):
            y_gather[u][d - 1].wait()
            far_forward[u][d].start()
        wait(near_forward[u])
        wait(far_forward[u])

    gather_near(0)
    gather_far(0)

    mine = pl.multiple_of(core * 64, 64)
    other = pl.multiple_of((1 - core) * 64, 64)

    def offsets(unit, first=0):
        return [
            [pl.multiple_of(first + me.coord_flip(axis, d) * unit, unit) for d in range(4)]
            for axis in range(3)
        ]

    rows_a, cols_b, cols_c = offsets(16, mine), offsets(512), offsets(128)
    cols_bc = [
        [pl.multiple_of(cols_b[b][0] + cols_c[c][0], 128) for c in range(3)] for b in range(3)
    ]

    def row_a(h, d=0):
        return rows_a[ORDERS[h][0]][d]

    def col_b(h, d=0):
        return cols_b[ORDERS[h][1]][d]

    def col_c(h, d=0):
        return cols_c[ORDERS[h][2]][d]

    def col_bc(h):
        return cols_bc[ORDERS[h][1]][ORDERS[h][2]]

    def piece(h, step):
        if step == 2:
            return wout.at[h, pl.ds(row_a(h), 16), pl.ds(col_bc(h), 128)]
        if step == 1:
            return wout.at[h, pl.ds(row_a(h), 16), pl.ds(col_b(h), 512)]
        return wout.at[h, pl.ds(row_a(h), 16), :]

    w_core, w_a, w_b, w_c, w_g, w_sib, w_out = [], [], [], [], [[], [], []], [], []
    for u in range(3):
        w_core.append(
            sems.copy(
                lambda u=u: wpart.at[span(u), pl.ds(other, 64), :],
                lambda u=u: wr0.at[span(u)],
                me.sibling,
            )
        )
        w_sib.append(
            sems.copy(
                lambda u=u: wout.at[span(u), pl.ds(mine, 64), :],
                lambda u=u: wout.at[span(u), pl.ds(mine, 64), :],
                me.sibling,
            )
        )
        w_out.append(
            pltpu.make_async_copy(wout.at[span(u)], wout_hbm.at[span(u)], store_sem.at[u])
        )
        w_a.append([
            sems.copy(
                lambda h=h, d=d: wpart.at[h, pl.ds(row_a(h, d), 16), :],
                lambda h=h, d=d: ra.at[d - 1, h],
                lambda h=h, d=d: me.along(ORDERS[h][0], d),
            )
            for h in heads(u) for d in range(1, 4)
        ])
        w_b.append([
            sems.copy(
                lambda h=h, d=d: sa.at[h, :, pl.ds(col_b(h, d), 512)],
                lambda h=h, d=d: rb.at[d - 1, h],
                lambda h=h, d=d: me.along(ORDERS[h][1], d),
            )
            for h in heads(u) for d in range(1, 4)
        ])
        w_c.append([
            sems.copy(
                lambda h=h, d=d: sb.at[h, :, pl.ds(col_c(h, d), 128)],
                lambda h=h, d=d: rc.at[d - 1, h],
                lambda h=h, d=d: me.along(ORDERS[h][2], d),
            )
            for h in heads(u) for d in range(1, 4)
        ])
        for step in range(3):
            w_g[step].append([
                sems.copy(
                    lambda h=h, step=step: piece(h, step),
                    lambda h=h, step=step: piece(h, step),
                    lambda h=h, d=d, step=step: me.along(ORDERS[h][step], d),
                )
                for h in heads(u) for d in range(1, 4)
            ])

    def weigh(u):
        def some(i, carry):
            c = pl.ds(pl.multiple_of(i * 512, 512), 512)
            part = dot(att[columns(u), :], go_ref[:, c], 1, 0)
            wpart[span(u), :, c] = part.reshape(UNITS[u][1], WIDTH, 512).astype(BF)
            return carry

        lax.fori_loop(0, COLS // 512, some, 0)
        w_core[u].start()

    def weight_core(u):
        w_core[u].wait()

        def some(h, carry):
            r = pl.ds(mine, 64)
            wpart[h, r, :] = (wpart[h, r, :].astype(F32) + wr0[h].astype(F32)).astype(BF)
            return carry

        lax.fori_loop(heads(u)[0], heads(u)[-1] + 1, some, 0)
        start(w_a[u])

    def weight_a(u):
        wait(w_a[u])
        for h in heads(u):
            t = wpart[h, pl.ds(row_a(h), 16), :].astype(F32)
            for d in range(3):
                t = t + ra[d, h].astype(F32)
            sa[h] = t.astype(BF)
        start(w_b[u])

    def weight_b(u):
        wait(w_b[u])
        for h in heads(u):
            t = sa[h, :, pl.ds(col_b(h), 512)].astype(F32)
            for d in range(3):
                t = t + rb[d, h].astype(F32)
            sb[h] = t.astype(BF)
        start(w_c[u])

    def weight_c(u):
        wait(w_c[u])
        for h in heads(u):
            t = sb[h, :, pl.ds(col_c(h), 128)].astype(F32)
            for d in range(3):
                t = t + rc[d, h].astype(F32)
            wout[h, pl.ds(row_a(h), 16), pl.ds(col_bc(h), 128)] = t.astype(BF)
        start(w_g[2][u])

    def weight_gather(u, step):
        wait(w_g[step][u])
        if step > 0:
            start(w_g[step - 1][u])
        else:
            w_sib[u].start()

    def weight_last(u):
        w_sib[u].wait()
        w_out[u].start()

    n_core, n_z, n_x, n_y = [], [], [], []
    for u in range(3):
        n_core.append(
            sems.copy(
                lambda u=u: gnf.at[:, pl.ds(HALF, HALF), columns(u)],
                lambda u=u: cr.at[:, :, columns(u)],
                me.sibling,
            )
        )
        n_z.append([
            sems.copy(
                lambda u=u, d=d: near_snd.at[:, :, d, :, columns(u)],
                lambda u=u, d=d: zr.at[d, :, :, :, columns(u)],
                lambda d=d: me.along(2, d),
            )
            for d in range(1, 4)
        ])
        n_x.append(
            sems.copy(
                lambda u=u: xs.at[:, :, columns(u)],
                lambda u=u: xr.at[:, :, columns(u)],
                lambda: me.chip(4),
            )
        )
        n_y.append([
            sems.copy(
                lambda u=u, d=d: far_snd.at[:, pl.ds(32 * d, 32), columns(u)],
                lambda u=u, d=d: yr.at[d, :, :, columns(u)],
                lambda d=d: me.along(1, d),
            )
            for d in range(1, 4)
        ])
    own_reduce = [
        sems.copy(lambda m=m: bxs.at[m], lambda m=m: bxr.at[m], lambda m=m: me.cross(m))
        for m in range(1, 16)
    ]

    def near_core(u):
        n_core[u].wait()
        cs = columns(u)
        for i in range(2):
            t = (gnf[i, 0:HALF, cs].astype(F32) + cr[i, :, cs].astype(F32)).astype(BF)
            for c in range(CHIPS):
                near_snd[i, c // 4, c % 4, :, cs] = t[32 * c : 32 * c + 32]
            far_snd[i, :, cs] = t[FAR:]
        start(n_z[u])
        start(n_y[u])

    def near_z(u):
        wait(n_z[u])
        cs = columns(u)
        for i in range(2):
            for x in range(2):
                t = near_snd[i, x, 0, :, cs].astype(F32)
                for d in range(1, 4):
                    t = t + zr[d, i, x, :, cs].astype(F32)
                if x == 0:
                    tot[i, :, cs] = t
                else:
                    xs[i, :, cs] = t.astype(BF)
        n_x[u].start()

    def near_x(u):
        n_x[u].wait()
        cs = columns(u)
        for i in range(2):
            tot[i, :, cs] = (tot[i, :, cs] + xr[i, :, cs].astype(F32)) * (1.0 / S1)

    def near_y(u):
        wait(n_y[u])
        cs = columns(u)
        for i in range(2):
            t = far_snd[i, 0:32, cs].astype(F32)
            for d in range(1, 4):
                t = t + yr[d, i, :, cs].astype(F32)
            xblk[i, :, cs] = t
        for part in ((), (0, 1, 2), (3,))[u]:
            for m in range(16):
                for i in range(2):
                    packed[m, 4 * part + 2 * i : 4 * part + 2 * i + 2, :] = xblk[
                        i, 2 * m : 2 * m + 2, part * 256 : part * 256 + 256
                    ]
        if u == 2:
            bxs[...] = packed[...].astype(BF)
            start(own_reduce)

    def finish_rows():
        wait(own_reduce)
        t = bxs[0].astype(F32)
        for m in range(1, 16):
            t = t + bxr[m].astype(F32)
        t = t * (1.0 / (S1 * S1))
        for i in range(2):
            for r in range(2):
                far_row = jnp.concatenate(
                    [t[4 * p + 2 * i + r : 4 * p + 2 * i + r + 1] for p in range(4)], axis=1
                )
                tot[i, 16 * r : 16 * r + 16, :] = tot[i, 16 * r : 16 * r + 16, :] + far_row

        def some(i, carry):
            r = pl.ds(pl.multiple_of(i * S1, S1), S1)
            k_ref[r, :] = (fine_k[r, :] + tot[0, pl.ds(i, 1), :]).astype(BF)
            v_ref[r, :] = (fine_v[r, :] + tot[1, pl.ds(i, 1), :]).astype(BF)
            return carry

        lax.fori_loop(0, ROWS // S1, some, 0, unroll=2)

    pair_row = lax.broadcasted_iota(jnp.int32, (32, ROWS), 0) // S1
    pair_col = lax.broadcasted_iota(jnp.int32, (32, ROWS), 1) // PAIR
    own_pair = pair_row == pair_col

    def forward(h):
        c = pl.ds(pl.multiple_of(h * WIDTH, WIDTH), WIDTH)
        qh = q_ref[:, c]
        s = dot(nf[0, :, c], qh, 1, 1)
        sf = [
            dot(k_ref[p * PAIR : (p + 1) * PAIR, c], qh[p * PAIR : (p + 1) * PAIR], 1, 1)
            for p in range(2)
        ]
        sf = jnp.concatenate(sf, axis=1)
        top = jnp.maximum(jnp.max(s, axis=0, keepdims=True), jnp.max(sf, axis=0, keepdims=True))
        e = jnp.exp2((s - top) * EXP2_SCALE)
        none = jnp.zeros((16, ROWS), F32)
        e = jnp.concatenate(
            [
                jnp.where(own_pair, 0.0, e[0:32]),
                e[32:FAR],
                none,
                e[FAR + 16 : HALF + FAR],
                none,
                e[HALF + FAR + 16 :],
            ],
            axis=0,
        )
        ef = jnp.exp2((sf - top) * EXP2_SCALE)
        total = jnp.sum(e, axis=0, keepdims=True) + jnp.sum(ef, axis=0, keepdims=True)
        e = e.astype(BF)
        ef = ef.astype(BF)
        probs[h, 0:KEYS, :] = e
        probs[h, KEYS : KEYS + PAIR, :] = ef
        out = dot(nf[1, :, c], e, 0, 0)
        of = [
            dot(v_ref[p * PAIR : (p + 1) * PAIR, c], ef[:, p * PAIR : (p + 1) * PAIR], 0, 0)
            for p in range(2)
        ]
        out = out + jnp.concatenate(of, axis=1)
        inv = 1.0 / total
        out = (out * inv).astype(BF)
        att[c, :] = out
        gth = gt[c, :].astype(F32)
        d = jnp.sum(out.astype(F32) * gth, axis=0, keepdims=True) * inv
        delta[h] = jnp.broadcast_to(d, (8, ROWS))
        scaled = gth * inv
        gst[c, :] = scaled.astype(BF)
        gs[:, c] = scaled.T.astype(BF)

    def backward(h):
        c = pl.ds(pl.multiple_of(h * WIDTH, WIDTH), WIDTH)
        qh = q_ref[:, c]
        gth = gst[c, :]
        gh = gs[:, c]
        d = delta[h, 0:1, :]
        e = probs[h, 0:KEYS, :]
        ds = (e.astype(F32) * (dot(nf[1, :, c], gth, 1, 0) - d)).astype(BF)
        gnf[1, :, c] = dot(e, gh, 1, 0).astype(BF)
        gnf[0, :, c] = (dot(ds, qh, 1, 0) * SCALE).astype(BF)
        dq = dot(nf[0, :, c], ds, 0, 0)
        dqf = []
        for p in range(2):
            r = slice(p * PAIR, (p + 1) * PAIR)
            ef = probs[h, KEYS : KEYS + PAIR, r]
            dsf = (ef.astype(F32) * (dot(v_ref[r, c], gth[:, r], 1, 0) - d[:, r])).astype(BF)
            fine_v[r, c] = dot(ef, gh[r], 1, 0)
            fine_k[r, c] = dot(dsf, qh[r], 1, 0) * SCALE
            dqf.append(dot(k_ref[r, c], dsf, 0, 0))
        dq = (dq + jnp.concatenate(dqf, axis=1)) * SCALE
        q_ref[:, c] = dq.T.astype(BF)

    def scheduled(work, plan):
        def step(h, carry):
            work(h)
            for at, actions in plan.items():

                @pl.when(h == at)
                def _():
                    for action, *args in actions:
                        action(*args)

            return carry

        lax.fori_loop(0, HEADS, step, 0)

    def near_send(u):
        n_core[u].start()

    scheduled(
        forward,
        {
            1: [(gather_near, 1)],
            2: [(gather_far, 1), (weigh, 0)],
            3: [(weight_core, 0)],
            4: [(gather_near, 2)],
            5: [(gather_far, 2), (weigh, 1)],
            6: [(weight_core, 1)],
            7: [(weight_a, 0), (weigh, 2)],
        },
    )
    scheduled(
        backward,
        {
            0: [(weight_core, 2)],
            1: [(weight_a, 1)],
            2: [(near_send, 0), (weight_b, 0)],
            3: [(near_core, 0), (weight_a, 2)],
            4: [(weight_b, 1)],
            5: [(near_send, 1), (weight_c, 0), (weight_b, 2)],
            6: [(near_core, 1), (weight_c, 1)],
            7: [(near_send, 2), (weight_c, 2), (weight_gather, 0, 2), (near_z, 0)],
        },
    )
    store_q = pltpu.make_async_copy(q_ref, gq_hbm, store_sem.at[3])
    store_q.start()
    near_core(2)
    weight_gather(1, 2)
    weight_gather(0, 1)
    weight_gather(2, 2)
    near_y(0)
    near_z(1)
    near_y(1)
    weight_gather(1, 1)
    near_y(2)
    weight_gather(2, 1)
    near_z(2)
    weight_gather(0, 0)
    near_x(0)
    near_x(1)
    weight_gather(1, 0)
    near_x(2)
    finish_rows()
    store_k = pltpu.make_async_copy(k_ref, gk_hbm, store_sem.at[4])
    store_v = pltpu.make_async_copy(v_ref, gv_hbm, store_sem.at[5])
    store_k.start()
    store_v.start()
    weight_last(0)
    weight_last(1)
    weight_gather(2, 0)
    weight_last(2)
    for copy in w_out + [store_q, store_k, store_v]:
        copy.wait()


def finish(
    scale, gq_in, gk_in, gv_in, w_in, gq_out, gk_out, gv_out, w_out,
    part, wide, kept, in_sem, out_sem,
):
    ins = [pltpu.make_async_copy(w_in.at[h], part.at[h], in_sem.at[h]) for h in range(HEADS)]
    outs = [
        pltpu.make_async_copy(wide.at[h], w_out.at[pl.ds(h * WIDTH, WIDTH)], out_sem.at[h])
        for h in range(HEADS)
    ]
    for i, (src, dst) in enumerate(((gq_in, gq_out), (gk_in, gk_out), (gv_in, gv_out))):
        ins.append(pltpu.make_async_copy(src, kept.at[i], in_sem.at[HEADS + i]))
        outs.append(pltpu.make_async_copy(kept.at[i], dst, out_sem.at[HEADS + i]))
    for copy in ins:
        copy.start()
    for h in range(HEADS):
        ins[h].wait()
        wide[h] = part[h].astype(F32) * scale
        outs[h].start()
    for i in range(HEADS, HEADS + 3):
        ins[i].wait()
        outs[i].start()
    for copy in outs:
        copy.wait()


def body(queries, key_rows, value_rows, grad_output, out_weight):
    vmem = pltpu.VMEM
    dma = pltpu.SemaphoreType.DMA
    scratch = [
        vmem((ROWS, ALL), BF),
        vmem((ROWS, ALL), BF),
        vmem((ROWS, ALL), BF),
        vmem((ROWS, COLS), BF),
        vmem((ALL, COLS), BF),
        vmem((2, KEYS, ALL), BF),
        vmem((16, 256), BF),
        vmem((16, 16, 256), BF),
        vmem((2, 32, ALL), F32),
        vmem((ALL, ROWS), BF),
        vmem((ALL, ROWS), BF),
        vmem((HEADS, KEYS + PAIR, ROWS), BF),
        vmem((ALL, ROWS), BF),
        vmem((ROWS, ALL), BF),
        vmem((HEADS, 8, ROWS), F32),
        vmem((2, KEYS, ALL), BF),
        vmem((2, HALF, ALL), BF),
        vmem((2, 2, 4, 32, ALL), BF),
        vmem((2, 128, ALL), BF),
        vmem((4, 2, 2, 32, ALL), BF),
        vmem((2, 32, ALL), BF),
        vmem((2, 32, ALL), BF),
        vmem((4, 2, 32, ALL), BF),
        vmem((16, 16, 256), F32),
        vmem((16, 16, 256), BF),
        vmem((16, 16, 256), BF),
        vmem((ROWS, ALL), F32),
        vmem((ROWS, ALL), F32),
        vmem((2, 32, ALL), F32),
        vmem((HEADS, WIDTH, COLS), BF),
        vmem((HEADS, 64, COLS), BF),
        vmem((3, HEADS, 16, COLS), BF),
        vmem((3, HEADS, 16, 512), BF),
        vmem((3, HEADS, 16, 128), BF),
        vmem((HEADS, 16, COLS), BF),
        vmem((HEADS, 16, 512), BF),
        vmem((HEADS, WIDTH, COLS), BF),
        dma((5,)),
        dma((6,)),
        dma((NSEM,)),
        dma((NSEM,)),
    ]
    hbm = pl.BlockSpec(memory_space=pl.ANY)
    token_shape = jax.ShapeDtypeStruct((ROWS, ALL), BF)
    grads = pl.pallas_call(
        kernel,
        out_shape=(token_shape,) * 3 + (jax.ShapeDtypeStruct((HEADS, WIDTH, COLS), BF),),
        in_specs=[hbm] * 5,
        out_specs=(hbm,) * 4,
        scratch_shapes=scratch,
        compiler_params=pltpu.CompilerParams(
            collective_id=0, has_side_effects=True, vmem_limit_bytes=64 * 1024 * 1024 - 65536
        ),
        name="fused",
    )(queries, key_rows, value_rows, grad_output, out_weight)
    tokens = ROWS * lax.axis_size("node") * lax.axis_size("group")
    return pl.pallas_call(
        functools.partial(finish, 1.0 / math.sqrt(tokens)),
        out_shape=(token_shape,) * 3 + (jax.ShapeDtypeStruct((ALL, COLS), F32),),
        in_specs=[hbm] * 4,
        out_specs=(hbm,) * 4,
        scratch_shapes=[
            vmem((HEADS, WIDTH, COLS), BF),
            vmem((HEADS, WIDTH, COLS), F32),
            vmem((3, ROWS, ALL), BF),
            dma((HEADS + 3,)),
            dma((HEADS + 3,)),
        ],
        compiler_params=pltpu.CompilerParams(vmem_limit_bytes=64 * 1024 * 1024 - 65536),
        name="finish",
    )(*grads)


def solution(mesh):
    split = P(("group", "node"), None)
    return jax.shard_map(
        body,
        mesh=mesh,
        in_specs=(split, split, split, split, P()),
        out_specs=(split, split, split, P()),
        check_vma=False,
    )
```

```python
import functools
import math

import jax
import jax.numpy as jnp
from jax import lax
from jax.experimental import pallas as pl
from jax.experimental.pallas import tpu as pltpu
from jax.sharding import PartitionSpec as P

HEADS = 8
WIDTH = 128
S1 = 16
ROWS = 512
PAIR = 256
CHIPS = 8
KEYS = 768
HALF = 384
FAR = 256
COLS = 2048
ALL = HEADS * WIDTH
UNITS = ((0, 3), (3, 3), (6, 2))
ORDERS = (
    (1, 0, 2), (0, 1, 2), (2, 0, 1), (1, 0, 2), (0, 1, 2), (2, 1, 0), (1, 2, 0), (0, 2, 1),
)
NSEM = 280
BF = jnp.bfloat16
F32 = jnp.float32
SCALE = 1.0 / math.sqrt(WIDTH)
EXP2_SCALE = math.log2(math.e) / math.sqrt(WIDTH)


def dot(a, b, ca, cb):
    return lax.dot_general(a, b, (((ca,), (cb,)), ((), ())), preferred_element_type=F32)


def flip4(a, d):
    if d == 0:
        return a
    if d == 1:
        return a + 1 - 2 * (a % 2)
    if d == 2:
        return (a + 2) % 4
    return 3 - a


def flip2(a, d):
    return 1 - a if d else a


class Place:
    def __init__(self):
        node = lax.axis_index("node")
        group = lax.axis_index("group")
        self.core = node % 2
        z = (node // 2) % 4
        x_lo = node // 8
        x_hi = group // 4
        y = group % 4
        los, his = [flip2(x_lo, d) for d in range(2)], [flip2(x_hi, d) for d in range(2)]
        zs, ys = [flip4(z, d) for d in range(4)], [flip4(y, d) for d in range(4)]
        self.flips = [[his[d // 2] * 2 + los[d % 2] for d in range(4)], ys, zs]
        self.sib = {"node": node + 1 - 2 * self.core, "group": group}
        self.crosses = [
            {"node": (los[m // 4 % 2] * 4 + zs[m % 4]) * 2 + self.core, "group": his[m // 8] * 4 + y}
            for m in range(16)
        ]
        self.ys = [{"node": node, "group": x_hi * 4 + ys[d]} for d in range(4)]

    def coord_flip(self, axis, d):
        return self.flips[axis][d]

    def sibling(self):
        return self.sib

    def cross(self, m):
        return self.crosses[m]

    def chip(self, c):
        return self.crosses[c]

    def along(self, axis, d):
        return (self.crosses[4 * d], self.ys[d], self.crosses[d])[axis]


class Sems:
    def __init__(self, send_sems, recv_sems):
        self.send_sems, self.recv_sems, self.used = send_sems, recv_sems, 0

    def copy(self, src, dst, device):
        i = self.used
        self.used += 1
        return Copy(src, dst, self.send_sems.at[i], self.recv_sems.at[i], device)


class Copy:
    def __init__(self, src, dst, send_sem, recv_sem, device):
        self.parts = src, dst, send_sem, recv_sem, device

    def make(self):
        src, dst, send_sem, recv_sem, device = self.parts
        return pltpu.make_async_remote_copy(
            src_ref=src(),
            dst_ref=dst(),
            send_sem=send_sem,
            recv_sem=recv_sem,
            device_id=device(),
            device_id_type=pl.DeviceIdType.MESH,
        )

    def start(self):
        self.make().start()

    def wait(self):
        self.make().wait()


def start(copies):
    for copy in copies:
        copy.start()


def wait(copies):
    for copy in copies:
        copy.wait()


def kernel(
    q_hbm, k_hbm, v_hbm, go_hbm, w_hbm,
    gq_hbm, gk_hbm, gv_hbm, wout_hbm,
    q_ref, k_ref, v_ref, go_ref, w_ref,
    nf, zsend, zrecv, xblk, gt, att, probs, gst, gs, delta,
    gnf, cr, near_snd, far_snd, zr, xs, xr, yr, packed, bxs, bxr, fine_k, fine_v, tot,
    wpart, wr0, ra, rb, rc, sa, sb, wout,
    load_sem, store_sem, send_sems, recv_sems,
):
    me = Place()
    core = me.core
    sems = Sems(send_sems, recv_sems)

    barrier = pltpu.get_barrier_semaphore()
    partners = [me.sibling()]
    partners += [me.cross(m) for m in range(1, 16)]
    partners += [me.along(1, d) for d in range(1, 4)]
    for partner in partners:
        pl.semaphore_signal(barrier, inc=1, device_id=partner, device_id_type=pl.DeviceIdType.MESH)

    loads = [
        pltpu.make_async_copy(src, dst, load_sem.at[i])
        for i, (src, dst) in enumerate(
            ((k_hbm, k_ref), (v_hbm, v_ref), (go_hbm, go_ref), (w_hbm, w_ref), (q_hbm, q_ref))
        )
    ]
    for load in loads:
        load.start()

    def heads(u):
        return range(UNITS[u][0], UNITS[u][0] + UNITS[u][1])

    def span(u):
        return pl.ds(*UNITS[u])

    def columns(u):
        return pl.ds(UNITS[u][0] * WIDTH, UNITS[u][1] * WIDTH)

    def near_at(c, u):
        return lambda: nf.at[:, pl.ds(32 * c, 32), columns(u)]

    def far_at(d, u):
        return lambda: nf.at[:, pl.ds(FAR + 32 * d, 32), columns(u)]

    def sib_at(first, u):
        return lambda: nf.at[:, pl.ds(HALF + first, 32), columns(u)]

    own_gather = [
        sems.copy(lambda: zsend, lambda m=m: zrecv.at[m], lambda m=m: me.cross(m))
        for m in range(1, 16)
    ]
    y_gather = [
        [sems.copy(far_at(0, u), far_at(d, u), lambda d=d: me.along(1, d)) for d in range(1, 4)]
        for u in range(3)
    ]
    near_gather = [
        [sems.copy(near_at(0, u), near_at(c, u), lambda c=c: me.chip(c)) for c in range(1, CHIPS)]
        for u in range(3)
    ]
    near_forward = [
        [sems.copy(near_at(c, u), sib_at(32 * c, u), me.sibling) for c in range(CHIPS)]
        for u in range(3)
    ]
    far_forward = [
        [sems.copy(far_at(d, u), sib_at(FAR + 32 * d, u), me.sibling) for d in range(4)]
        for u in range(3)
    ]

    rows = lax.broadcasted_iota(jnp.int32, (32, ROWS), 0)
    toks = lax.broadcasted_iota(jnp.int32, (32, ROWS), 1)
    mean16 = jnp.where(toks // S1 == rows, 1.0 / S1, 0.0).astype(BF)
    r8 = lax.broadcasted_iota(jnp.int32, (8, 32), 0)
    c8 = lax.broadcasted_iota(jnp.int32, (8, 32), 1) // 16
    pick_k = jnp.where(c8 == r8, 1.0 / S1, 0.0).astype(BF)
    pick_v = jnp.where(c8 + 2 == r8, 1.0 / S1, 0.0).astype(BF)
    loads[0].wait()
    near_k = dot(mean16, k_ref[...], 1, 0).astype(BF)
    nf[0, 0:32, :] = near_k
    loads[1].wait()
    near_v = dot(mean16, v_ref[...], 1, 0).astype(BF)
    nf[1, 0:32, :] = near_v
    far_own = (dot(pick_k, near_k, 1, 0) + dot(pick_v, near_v, 1, 0)).astype(BF).astype(F32)
    zsend[...] = jnp.concatenate(
        [far_own[0:4, 256 * part : 256 * part + 256] for part in range(4)], axis=0
    ).astype(BF)

    pl.semaphore_wait(barrier, len(partners))
    start(own_gather)
    for u in range(3):
        start(near_gather[u])
        near_forward[u][0].start()

    def project(i, carry):
        r = pl.ds(pl.multiple_of(i * 256, 256), 256)
        gt[r, :] = dot(w_ref[r, :], go_ref[...], 1, 1).astype(BF)
        return carry

    loads[2].wait()
    loads[3].wait()
    lax.fori_loop(0, 4, project, 0)

    wait(own_gather)
    for m in range(16):
        block = (zsend[...] if m == 0 else zrecv[m]).astype(F32)
        for i in range(2):
            for part in range(4):
                xblk[i, 2 * m : 2 * m + 2, part * 256 : part * 256 + 256] = block[
                    4 * part + 2 * i : 4 * part + 2 * i + 2
                ]
    nf[:, FAR : FAR + 32, :] = xblk[...].astype(BF)
    for u in range(3):
        start(y_gather[u])
        far_forward[u][0].start()
    loads[4].wait()

    def gather_near(u):
        for c in range(1, CHIPS):
            near_gather[u][c - 1].wait()
            near_forward[u][c].start()

    def gather_far(u):
        for d in range(1, 4):
            y_gather[u][d - 1].wait()
            far_forward[u][d].start()
        wait(near_forward[u])
        wait(far_forward[u])

    gather_near(0)
    gather_far(0)

    mine = pl.multiple_of(core * 64, 64)
    other = pl.multiple_of((1 - core) * 64, 64)

    def offsets(unit, first=0):
        return [
            [pl.multiple_of(first + me.coord_flip(axis, d) * unit, unit) for d in range(4)]
            for axis in range(3)
        ]

    rows_a, cols_b, cols_c = offsets(16, mine), offsets(512), offsets(128)
    cols_bc = [
        [pl.multiple_of(cols_b[b][0] + cols_c[c][0], 128) for c in range(3)] for b in range(3)
    ]

    def row_a(h, d=0):
        return rows_a[ORDERS[h][0]][d]

    def col_b(h, d=0):
        return cols_b[ORDERS[h][1]][d]

    def col_c(h, d=0):
        return cols_c[ORDERS[h][2]][d]

    def col_bc(h):
        return cols_bc[ORDERS[h][1]][ORDERS[h][2]]

    def piece(h, step):
        if step == 2:
            return wout.at[h, pl.ds(row_a(h), 16), pl.ds(col_bc(h), 128)]
        if step == 1:
            return wout.at[h, pl.ds(row_a(h), 16), pl.ds(col_b(h), 512)]
        return wout.at[h, pl.ds(row_a(h), 16), :]

    w_core, w_a, w_b, w_c, w_g, w_sib, w_out = [], [], [], [], [[], [], []], [], []
    for u in range(3):
        w_core.append(
            sems.copy(
                lambda u=u: wpart.at[span(u), pl.ds(other, 64), :],
                lambda u=u: wr0.at[span(u)],
                me.sibling,
            )
        )
        w_sib.append(
            sems.copy(
                lambda u=u: wout.at[span(u), pl.ds(mine, 64), :],
                lambda u=u: wout.at[span(u), pl.ds(mine, 64), :],
                me.sibling,
            )
        )
        w_out.append(
            pltpu.make_async_copy(wout.at[span(u)], wout_hbm.at[span(u)], store_sem.at[u])
        )
        w_a.append([
            sems.copy(
                lambda h=h, d=d: wpart.at[h, pl.ds(row_a(h, d), 16), :],
                lambda h=h, d=d: ra.at[d - 1, h],
                lambda h=h, d=d: me.along(ORDERS[h][0], d),
            )
            for h in heads(u) for d in range(1, 4)
        ])
        w_b.append([
            sems.copy(
                lambda h=h, d=d: sa.at[h, :, pl.ds(col_b(h, d), 512)],
                lambda h=h, d=d: rb.at[d - 1, h],
                lambda h=h, d=d: me.along(ORDERS[h][1], d),
            )
            for h in heads(u) for d in range(1, 4)
        ])
        w_c.append([
            sems.copy(
                lambda h=h, d=d: sb.at[h, :, pl.ds(col_c(h, d), 128)],
                lambda h=h, d=d: rc.at[d - 1, h],
                lambda h=h, d=d: me.along(ORDERS[h][2], d),
            )
            for h in heads(u) for d in range(1, 4)
        ])
        for step in range(3):
            w_g[step].append([
                sems.copy(
                    lambda h=h, step=step: piece(h, step),
                    lambda h=h, step=step: piece(h, step),
                    lambda h=h, d=d, step=step: me.along(ORDERS[h][step], d),
                )
                for h in heads(u) for d in range(1, 4)
            ])

    def weigh(u):
        def some(i, carry):
            c = pl.ds(pl.multiple_of(i * 512, 512), 512)
            part = dot(att[columns(u), :], go_ref[:, c], 1, 0)
            wpart[span(u), :, c] = part.reshape(UNITS[u][1], WIDTH, 512).astype(BF)
            return carry

        lax.fori_loop(0, COLS // 512, some, 0)
        w_core[u].start()

    def weight_core(u):
        w_core[u].wait()

        def some(h, carry):
            r = pl.ds(mine, 64)
            wpart[h, r, :] = (wpart[h, r, :].astype(F32) + wr0[h].astype(F32)).astype(BF)
            return carry

        lax.fori_loop(heads(u)[0], heads(u)[-1] + 1, some, 0)
        start(w_a[u])

    def weight_a(u):
        wait(w_a[u])
        for h in heads(u):
            t = wpart[h, pl.ds(row_a(h), 16), :].astype(F32)
            for d in range(3):
                t = t + ra[d, h].astype(F32)
            sa[h] = t.astype(BF)
        start(w_b[u])

    def weight_b(u):
        wait(w_b[u])
        for h in heads(u):
            t = sa[h, :, pl.ds(col_b(h), 512)].astype(F32)
            for d in range(3):
                t = t + rb[d, h].astype(F32)
            sb[h] = t.astype(BF)
        start(w_c[u])

    def weight_c(u):
        wait(w_c[u])
        for h in heads(u):
            t = sb[h, :, pl.ds(col_c(h), 128)].astype(F32)
            for d in range(3):
                t = t + rc[d, h].astype(F32)
            wout[h, pl.ds(row_a(h), 16), pl.ds(col_bc(h), 128)] = t.astype(BF)
        start(w_g[2][u])

    def weight_gather(u, step):
        wait(w_g[step][u])
        if step > 0:
            start(w_g[step - 1][u])
        else:
            w_sib[u].start()

    def weight_last(u):
        w_sib[u].wait()
        w_out[u].start()

    n_core, n_z, n_x, n_y = [], [], [], []
    for u in range(3):
        n_core.append(
            sems.copy(
                lambda u=u: gnf.at[:, pl.ds(HALF, HALF), columns(u)],
                lambda u=u: cr.at[:, :, columns(u)],
                me.sibling,
            )
        )
        n_z.append([
            sems.copy(
                lambda u=u, d=d: near_snd.at[:, :, d, :, columns(u)],
                lambda u=u, d=d: zr.at[d, :, :, :, columns(u)],
                lambda d=d: me.along(2, d),
            )
            for d in range(1, 4)
        ])
        n_x.append(
            sems.copy(
                lambda u=u: xs.at[:, :, columns(u)],
                lambda u=u: xr.at[:, :, columns(u)],
                lambda: me.chip(4),
            )
        )
        n_y.append([
            sems.copy(
                lambda u=u, d=d: far_snd.at[:, pl.ds(32 * d, 32), columns(u)],
                lambda u=u, d=d: yr.at[d, :, :, columns(u)],
                lambda d=d: me.along(1, d),
            )
            for d in range(1, 4)
        ])
    own_reduce = [
        sems.copy(lambda m=m: bxs.at[m], lambda m=m: bxr.at[m], lambda m=m: me.cross(m))
        for m in range(1, 16)
    ]

    def near_core(u):
        n_core[u].wait()
        cs = columns(u)
        for i in range(2):
            t = (gnf[i, 0:HALF, cs].astype(F32) + cr[i, :, cs].astype(F32)).astype(BF)
            for c in range(CHIPS):
                near_snd[i, c // 4, c % 4, :, cs] = t[32 * c : 32 * c + 32]
            far_snd[i, :, cs] = t[FAR:]
        start(n_z[u])
        start(n_y[u])

    def near_z(u):
        wait(n_z[u])
        cs = columns(u)
        for i in range(2):
            for x in range(2):
                t = near_snd[i, x, 0, :, cs].astype(F32)
                for d in range(1, 4):
                    t = t + zr[d, i, x, :, cs].astype(F32)
                if x == 0:
                    tot[i, :, cs] = t
                else:
                    xs[i, :, cs] = t.astype(BF)
        n_x[u].start()

    def near_x(u):
        n_x[u].wait()
        cs = columns(u)
        for i in range(2):
            tot[i, :, cs] = (tot[i, :, cs] + xr[i, :, cs].astype(F32)) * (1.0 / S1)

    def near_y(u):
        wait(n_y[u])
        cs = columns(u)
        for i in range(2):
            t = far_snd[i, 0:32, cs].astype(F32)
            for d in range(1, 4):
                t = t + yr[d, i, :, cs].astype(F32)
            xblk[i, :, cs] = t
        for part in ((), (0, 1, 2), (3,))[u]:
            for m in range(16):
                for i in range(2):
                    packed[m, 4 * part + 2 * i : 4 * part + 2 * i + 2, :] = xblk[
                        i, 2 * m : 2 * m + 2, part * 256 : part * 256 + 256
                    ]
        if u == 2:
            bxs[...] = packed[...].astype(BF)
            start(own_reduce)

    def finish_rows():
        wait(own_reduce)
        t = bxs[0].astype(F32)
        for m in range(1, 16):
            t = t + bxr[m].astype(F32)
        t = t * (1.0 / (S1 * S1))
        for i in range(2):
            for r in range(2):
                far_row = jnp.concatenate(
                    [t[4 * p + 2 * i + r : 4 * p + 2 * i + r + 1] for p in range(4)], axis=1
                )
                tot[i, 16 * r : 16 * r + 16, :] = tot[i, 16 * r : 16 * r + 16, :] + far_row

        def some(i, carry):
            r = pl.ds(pl.multiple_of(i * S1, S1), S1)
            k_ref[r, :] = (fine_k[r, :] + tot[0, pl.ds(i, 1), :]).astype(BF)
            v_ref[r, :] = (fine_v[r, :] + tot[1, pl.ds(i, 1), :]).astype(BF)
            return carry

        lax.fori_loop(0, ROWS // S1, some, 0, unroll=2)

    pair_row = lax.broadcasted_iota(jnp.int32, (32, ROWS), 0) // S1
    pair_col = lax.broadcasted_iota(jnp.int32, (32, ROWS), 1) // PAIR
    own_pair = pair_row == pair_col

    def forward(h):
        c = pl.ds(pl.multiple_of(h * WIDTH, WIDTH), WIDTH)
        qh = q_ref[:, c]
        s = dot(nf[0, :, c], qh, 1, 1)
        sf = [
            dot(k_ref[p * PAIR : (p + 1) * PAIR, c], qh[p * PAIR : (p + 1) * PAIR], 1, 1)
            for p in range(2)
        ]
        sf = jnp.concatenate(sf, axis=1)
        top = jnp.maximum(jnp.max(s, axis=0, keepdims=True), jnp.max(sf, axis=0, keepdims=True))
        e = jnp.exp2((s - top) * EXP2_SCALE)
        none = jnp.zeros((16, ROWS), F32)
        e = jnp.concatenate(
            [
                jnp.where(own_pair, 0.0, e[0:32]),
                e[32:FAR],
                none,
                e[FAR + 16 : HALF + FAR],
                none,
                e[HALF + FAR + 16 :],
            ],
            axis=0,
        )
        ef = jnp.exp2((sf - top) * EXP2_SCALE)
        total = jnp.sum(e, axis=0, keepdims=True) + jnp.sum(ef, axis=0, keepdims=True)
        e = e.astype(BF)
        ef = ef.astype(BF)
        probs[h, 0:KEYS, :] = e
        probs[h, KEYS : KEYS + PAIR, :] = ef
        out = dot(nf[1, :, c], e, 0, 0)
        of = [
            dot(v_ref[p * PAIR : (p + 1) * PAIR, c], ef[:, p * PAIR : (p + 1) * PAIR], 0, 0)
            for p in range(2)
        ]
        out = out + jnp.concatenate(of, axis=1)
        inv = 1.0 / total
        out = (out * inv).astype(BF)
        att[c, :] = out
        gth = gt[c, :].astype(F32)
        d = jnp.sum(out.astype(F32) * gth, axis=0, keepdims=True) * inv
        delta[h] = jnp.broadcast_to(d, (8, ROWS))
        scaled = gth * inv
        gst[c, :] = scaled.astype(BF)
        gs[:, c] = scaled.T.astype(BF)

    def backward(h):
        c = pl.ds(pl.multiple_of(h * WIDTH, WIDTH), WIDTH)
        qh = q_ref[:, c]
        gth = gst[c, :]
        gh = gs[:, c]
        d = delta[h, 0:1, :]
        e = probs[h, 0:KEYS, :]
        ds = (e.astype(F32) * (dot(nf[1, :, c], gth, 1, 0) - d)).astype(BF)
        gnf[1, :, c] = dot(e, gh, 1, 0).astype(BF)
        gnf[0, :, c] = (dot(ds, qh, 1, 0) * SCALE).astype(BF)
        dq = dot(nf[0, :, c], ds, 0, 0)
        dqf = []
        for p in range(2):
            r = slice(p * PAIR, (p + 1) * PAIR)
            ef = probs[h, KEYS : KEYS + PAIR, r]
            dsf = (ef.astype(F32) * (dot(v_ref[r, c], gth[:, r], 1, 0) - d[:, r])).astype(BF)
            fine_v[r, c] = dot(ef, gh[r], 1, 0)
            fine_k[r, c] = dot(dsf, qh[r], 1, 0) * SCALE
            dqf.append(dot(k_ref[r, c], dsf, 0, 0))
        dq = (dq + jnp.concatenate(dqf, axis=1)) * SCALE
        q_ref[:, c] = dq.T.astype(BF)

    def scheduled(work, plan):
        def step(h, carry):
            work(h)
            for at, actions in plan.items():

                @pl.when(h == at)
                def _():
                    for action, *args in actions:
                        action(*args)

            return carry

        lax.fori_loop(0, HEADS, step, 0)

    def near_send(u):
        n_core[u].start()

    scheduled(
        forward,
        {
            1: [(gather_near, 1)],
            2: [(gather_far, 1), (weigh, 0)],
            3: [(weight_core, 0)],
            4: [(gather_near, 2)],
            5: [(gather_far, 2), (weigh, 1)],
            6: [(weight_core, 1)],
            7: [(weight_a, 0), (weigh, 2)],
        },
    )
    scheduled(
        backward,
        {
            0: [(weight_core, 2)],
            1: [(weight_a, 1), (weight_b, 0)],
            2: [(near_send, 0)],
            3: [(weight_c, 0), (weight_a, 2), (weight_b, 1), (near_core, 0)],
            5: [(near_send, 1), (weight_gather, 0, 2), (weight_c, 1), (weight_b, 2)],
            6: [(near_core, 1)],
            7: [
                (near_send, 2), (weight_gather, 0, 1), (weight_gather, 1, 2), (weight_c, 2),
                (near_z, 0),
            ],
        },
    )
    store_q = pltpu.make_async_copy(q_ref, gq_hbm, store_sem.at[3])
    store_q.start()
    near_core(2)
    weight_gather(2, 2)
    weight_gather(1, 1)
    near_y(0)
    near_z(1)
    near_y(1)
    weight_gather(2, 1)
    near_y(2)
    weight_gather(0, 0)
    near_z(2)
    near_x(0)
    near_x(1)
    weight_gather(1, 0)
    near_x(2)
    finish_rows()
    store_k = pltpu.make_async_copy(k_ref, gk_hbm, store_sem.at[4])
    store_v = pltpu.make_async_copy(v_ref, gv_hbm, store_sem.at[5])
    store_k.start()
    store_v.start()
    weight_last(0)
    weight_last(1)
    weight_gather(2, 0)
    weight_last(2)
    for copy in w_out + [store_q, store_k, store_v]:
        copy.wait()


def finish(
    scale, gq_in, gk_in, gv_in, w_in, gq_out, gk_out, gv_out, w_out,
    part, wide, kept, in_sem, out_sem,
):
    ins = [pltpu.make_async_copy(w_in.at[h], part.at[h], in_sem.at[h]) for h in range(HEADS)]
    outs = [
        pltpu.make_async_copy(wide.at[h], w_out.at[pl.ds(h * WIDTH, WIDTH)], out_sem.at[h])
        for h in range(HEADS)
    ]
    for i, (src, dst) in enumerate(((gq_in, gq_out), (gk_in, gk_out), (gv_in, gv_out))):
        ins.append(pltpu.make_async_copy(src, kept.at[i], in_sem.at[HEADS + i]))
        outs.append(pltpu.make_async_copy(kept.at[i], dst, out_sem.at[HEADS + i]))
    for copy in ins:
        copy.start()
    for h in range(HEADS):
        ins[h].wait()
        wide[h] = part[h].astype(F32) * scale
        outs[h].start()
    for i in range(HEADS, HEADS + 3):
        ins[i].wait()
        outs[i].start()
    for copy in outs:
        copy.wait()


def body(queries, key_rows, value_rows, grad_output, out_weight):
    vmem = pltpu.VMEM
    dma = pltpu.SemaphoreType.DMA
    scratch = [
        vmem((ROWS, ALL), BF),
        vmem((ROWS, ALL), BF),
        vmem((ROWS, ALL), BF),
        vmem((ROWS, COLS), BF),
        vmem((ALL, COLS), BF),
        vmem((2, KEYS, ALL), BF),
        vmem((16, 256), BF),
        vmem((16, 16, 256), BF),
        vmem((2, 32, ALL), F32),
        vmem((ALL, ROWS), BF),
        vmem((ALL, ROWS), BF),
        vmem((HEADS, KEYS + PAIR, ROWS), BF),
        vmem((ALL, ROWS), BF),
        vmem((ROWS, ALL), BF),
        vmem((HEADS, 8, ROWS), F32),
        vmem((2, KEYS, ALL), BF),
        vmem((2, HALF, ALL), BF),
        vmem((2, 2, 4, 32, ALL), BF),
        vmem((2, 128, ALL), BF),
        vmem((4, 2, 2, 32, ALL), BF),
        vmem((2, 32, ALL), BF),
        vmem((2, 32, ALL), BF),
        vmem((4, 2, 32, ALL), BF),
        vmem((16, 16, 256), F32),
        vmem((16, 16, 256), BF),
        vmem((16, 16, 256), BF),
        vmem((ROWS, ALL), F32),
        vmem((ROWS, ALL), F32),
        vmem((2, 32, ALL), F32),
        vmem((HEADS, WIDTH, COLS), BF),
        vmem((HEADS, 64, COLS), BF),
        vmem((3, HEADS, 16, COLS), BF),
        vmem((3, HEADS, 16, 512), BF),
        vmem((3, HEADS, 16, 128), BF),
        vmem((HEADS, 16, COLS), BF),
        vmem((HEADS, 16, 512), BF),
        vmem((HEADS, WIDTH, COLS), BF),
        dma((5,)),
        dma((6,)),
        dma((NSEM,)),
        dma((NSEM,)),
    ]
    hbm = pl.BlockSpec(memory_space=pl.ANY)
    token_shape = jax.ShapeDtypeStruct((ROWS, ALL), BF)
    grads = pl.pallas_call(
        kernel,
        out_shape=(token_shape,) * 3 + (jax.ShapeDtypeStruct((HEADS, WIDTH, COLS), BF),),
        in_specs=[hbm] * 5,
        out_specs=(hbm,) * 4,
        scratch_shapes=scratch,
        compiler_params=pltpu.CompilerParams(
            collective_id=0, has_side_effects=True, vmem_limit_bytes=64 * 1024 * 1024 - 65536
        ),
        name="fused",
    )(queries, key_rows, value_rows, grad_output, out_weight)
    tokens = ROWS * lax.axis_size("node") * lax.axis_size("group")
    return pl.pallas_call(
        functools.partial(finish, 1.0 / math.sqrt(tokens)),
        out_shape=(token_shape,) * 3 + (jax.ShapeDtypeStruct((ALL, COLS), F32),),
        in_specs=[hbm] * 4,
        out_specs=(hbm,) * 4,
        scratch_shapes=[
            vmem((HEADS, WIDTH, COLS), BF),
            vmem((HEADS, WIDTH, COLS), F32),
            vmem((3, ROWS, ALL), BF),
            dma((HEADS + 3,)),
            dma((HEADS + 3,)),
        ],
        compiler_params=pltpu.CompilerParams(vmem_limit_bytes=64 * 1024 * 1024 - 65536),
        name="finish",
    )(*grads)


def solution(mesh):
    split = P(("group", "node"), None)
    return jax.shard_map(
        body,
        mesh=mesh,
        in_specs=(split, split, split, split, P()),
        out_specs=(split, split, split, P()),
        check_vma=False,
    )
```

```python
import functools
import math

import jax
import jax.numpy as jnp
from jax import lax
from jax.experimental import pallas as pl
from jax.experimental.pallas import tpu as pltpu
from jax.sharding import PartitionSpec as P

HEADS = 8
WIDTH = 128
S1 = 16
ROWS = 512
PAIR = 256
CHIPS = 8
KEYS = 768
HALF = 384
FAR = 256
COLS = 2048
ALL = HEADS * WIDTH
UNITS = ((0, 3), (3, 3), (6, 2))
ORDERS = (
    (1, 0, 2), (0, 1, 2), (2, 0, 1), (1, 0, 2), (0, 1, 2), (2, 1, 0), (1, 2, 0), (0, 2, 1),
)
NSEM = 280
BF = jnp.bfloat16
F32 = jnp.float32
SCALE = 1.0 / math.sqrt(WIDTH)
EXP2_SCALE = math.log2(math.e) / math.sqrt(WIDTH)


def dot(a, b, ca, cb):
    return lax.dot_general(a, b, (((ca,), (cb,)), ((), ())), preferred_element_type=F32)


def flip4(a, d):
    if d == 0:
        return a
    if d == 1:
        return a + 1 - 2 * (a % 2)
    if d == 2:
        return (a + 2) % 4
    return 3 - a


def flip2(a, d):
    return 1 - a if d else a


class Place:
    def __init__(self):
        node = lax.axis_index("node")
        group = lax.axis_index("group")
        self.core = node % 2
        z = (node // 2) % 4
        x_lo = node // 8
        x_hi = group // 4
        y = group % 4
        los, his = [flip2(x_lo, d) for d in range(2)], [flip2(x_hi, d) for d in range(2)]
        zs, ys = [flip4(z, d) for d in range(4)], [flip4(y, d) for d in range(4)]
        self.flips = [[his[d // 2] * 2 + los[d % 2] for d in range(4)], ys, zs]
        self.sib = {"node": node + 1 - 2 * self.core, "group": group}
        self.crosses = [
            {"node": (los[m // 4 % 2] * 4 + zs[m % 4]) * 2 + self.core, "group": his[m // 8] * 4 + y}
            for m in range(16)
        ]
        self.ys = [{"node": node, "group": x_hi * 4 + ys[d]} for d in range(4)]

    def coord_flip(self, axis, d):
        return self.flips[axis][d]

    def sibling(self):
        return self.sib

    def cross(self, m):
        return self.crosses[m]

    def chip(self, c):
        return self.crosses[c]

    def along(self, axis, d):
        return (self.crosses[4 * d], self.ys[d], self.crosses[d])[axis]


class Sems:
    def __init__(self, send_sems, recv_sems):
        self.send_sems, self.recv_sems, self.used = send_sems, recv_sems, 0

    def copy(self, src, dst, device):
        i = self.used
        self.used += 1
        return Copy(src, dst, self.send_sems.at[i], self.recv_sems.at[i], device)


class Copy:
    def __init__(self, src, dst, send_sem, recv_sem, device):
        self.parts = src, dst, send_sem, recv_sem, device

    def make(self):
        src, dst, send_sem, recv_sem, device = self.parts
        return pltpu.make_async_remote_copy(
            src_ref=src(),
            dst_ref=dst(),
            send_sem=send_sem,
            recv_sem=recv_sem,
            device_id=device(),
            device_id_type=pl.DeviceIdType.MESH,
        )

    def start(self):
        self.make().start()

    def wait(self):
        self.make().wait()


def start(copies):
    for copy in copies:
        copy.start()


def wait(copies):
    for copy in copies:
        copy.wait()


def kernel(
    q_hbm, k_hbm, v_hbm, go_hbm, w_hbm,
    gq_hbm, gk_hbm, gv_hbm, wout_hbm,
    q_ref, k_ref, v_ref, go_ref, w_ref,
    nf, zsend, zrecv, xblk, gt, att, probs, gst, gs, delta,
    gnf, cr, near_snd, far_snd, zr, xs, xr, yr, packed, bxs, bxr, fine_k, fine_v, tot,
    wpart, wr0, ra, rb, rc, sa, sb, wout,
    load_sem, store_sem, send_sems, recv_sems,
):
    me = Place()
    core = me.core
    sems = Sems(send_sems, recv_sems)

    barrier = pltpu.get_barrier_semaphore()
    partners = [me.sibling()]
    partners += [me.cross(m) for m in range(1, 16)]
    partners += [me.along(1, d) for d in range(1, 4)]
    for partner in partners:
        pl.semaphore_signal(barrier, inc=1, device_id=partner, device_id_type=pl.DeviceIdType.MESH)

    loads = [
        pltpu.make_async_copy(src, dst, load_sem.at[i])
        for i, (src, dst) in enumerate(
            ((k_hbm, k_ref), (v_hbm, v_ref), (go_hbm, go_ref), (w_hbm, w_ref), (q_hbm, q_ref))
        )
    ]
    for load in loads:
        load.start()

    def heads(u):
        return range(UNITS[u][0], UNITS[u][0] + UNITS[u][1])

    def span(u):
        return pl.ds(*UNITS[u])

    def columns(u):
        return pl.ds(UNITS[u][0] * WIDTH, UNITS[u][1] * WIDTH)

    def near_at(c, u):
        return lambda: nf.at[:, pl.ds(32 * c, 32), columns(u)]

    def far_at(d, u):
        return lambda: nf.at[:, pl.ds(FAR + 32 * d, 32), columns(u)]

    def sib_at(first, u):
        return lambda: nf.at[:, pl.ds(HALF + first, 32), columns(u)]

    own_gather = [
        sems.copy(lambda: zsend, lambda m=m: zrecv.at[m], lambda m=m: me.cross(m))
        for m in range(1, 16)
    ]
    y_gather = [
        [sems.copy(far_at(0, u), far_at(d, u), lambda d=d: me.along(1, d)) for d in range(1, 4)]
        for u in range(3)
    ]
    near_gather = [
        [sems.copy(near_at(0, u), near_at(c, u), lambda c=c: me.chip(c)) for c in range(1, 5)]
        + [sems.copy(near_at(4, u), near_at(4 + d, u), lambda d=d: me.along(2, d)) for d in range(1, 4)]
        for u in range(3)
    ]
    near_forward = [
        [sems.copy(near_at(c, u), sib_at(32 * c, u), me.sibling) for c in range(CHIPS)]
        for u in range(3)
    ]
    far_forward = [
        [sems.copy(far_at(d, u), sib_at(FAR + 32 * d, u), me.sibling) for d in range(4)]
        for u in range(3)
    ]

    rows = lax.broadcasted_iota(jnp.int32, (32, ROWS), 0)
    toks = lax.broadcasted_iota(jnp.int32, (32, ROWS), 1)
    mean16 = jnp.where(toks // S1 == rows, 1.0 / S1, 0.0).astype(BF)
    r8 = lax.broadcasted_iota(jnp.int32, (8, 32), 0)
    c8 = lax.broadcasted_iota(jnp.int32, (8, 32), 1) // 16
    pick_k = jnp.where(c8 == r8, 1.0 / S1, 0.0).astype(BF)
    pick_v = jnp.where(c8 + 2 == r8, 1.0 / S1, 0.0).astype(BF)
    loads[0].wait()
    near_k = dot(mean16, k_ref[...], 1, 0).astype(BF)
    nf[0, 0:32, :] = near_k
    loads[1].wait()
    near_v = dot(mean16, v_ref[...], 1, 0).astype(BF)
    nf[1, 0:32, :] = near_v
    far_own = (dot(pick_k, near_k, 1, 0) + dot(pick_v, near_v, 1, 0)).astype(BF).astype(F32)
    zsend[...] = jnp.concatenate(
        [far_own[0:4, 256 * part : 256 * part + 256] for part in range(4)], axis=0
    ).astype(BF)

    pl.semaphore_wait(barrier, len(partners))
    start(own_gather)
    for u in range(3):
        start(near_gather[u][:4])
        near_forward[u][0].start()

    def project(i, carry):
        r = pl.ds(pl.multiple_of(i * 256, 256), 256)
        gt[r, :] = dot(w_ref[r, :], go_ref[...], 1, 1).astype(BF)
        return carry

    loads[2].wait()
    loads[3].wait()
    lax.fori_loop(0, 4, project, 0)

    def relay(u):
        near_gather[u][3].wait()
        start(near_gather[u][4:])
        near_forward[u][4].start()

    relay(0)

    wait(own_gather)
    for m in range(16):
        block = (zsend[...] if m == 0 else zrecv[m]).astype(F32)
        for i in range(2):
            for part in range(4):
                xblk[i, 2 * m : 2 * m + 2, part * 256 : part * 256 + 256] = block[
                    4 * part + 2 * i : 4 * part + 2 * i + 2
                ]
    nf[:, FAR : FAR + 32, :] = xblk[...].astype(BF)
    for u in range(3):
        start(y_gather[u])
        far_forward[u][0].start()
    loads[4].wait()
    relay(1)
    relay(2)

    def gather_near(u):
        for c in (1, 2, 3, 5, 6, 7):
            near_gather[u][c - 1].wait()
            near_forward[u][c].start()

    def gather_far(u):
        for d in range(1, 4):
            y_gather[u][d - 1].wait()
            far_forward[u][d].start()
        wait(near_forward[u])
        wait(far_forward[u])

    gather_near(0)
    gather_far(0)

    mine = pl.multiple_of(core * 64, 64)
    other = pl.multiple_of((1 - core) * 64, 64)

    def offsets(unit, first=0):
        return [
            [pl.multiple_of(first + me.coord_flip(axis, d) * unit, unit) for d in range(4)]
            for axis in range(3)
        ]

    rows_a, cols_b, cols_c = offsets(16, mine), offsets(512), offsets(128)
    cols_bc = [
        [pl.multiple_of(cols_b[b][0] + cols_c[c][0], 128) for c in range(3)] for b in range(3)
    ]

    def row_a(h, d=0):
        return rows_a[ORDERS[h][0]][d]

    def col_b(h, d=0):
        return cols_b[ORDERS[h][1]][d]

    def col_c(h, d=0):
        return cols_c[ORDERS[h][2]][d]

    def col_bc(h):
        return cols_bc[ORDERS[h][1]][ORDERS[h][2]]

    def piece(h, step):
        if step == 2:
            return wout.at[h, pl.ds(row_a(h), 16), pl.ds(col_bc(h), 128)]
        if step == 1:
            return wout.at[h, pl.ds(row_a(h), 16), pl.ds(col_b(h), 512)]
        return wout.at[h, pl.ds(row_a(h), 16), :]

    w_core, w_a, w_b, w_c, w_g, w_sib, w_out = [], [], [], [], [[], [], []], [], []
    for u in range(3):
        w_core.append(
            sems.copy(
                lambda u=u: wpart.at[span(u), pl.ds(other, 64), :],
                lambda u=u: wr0.at[span(u)],
                me.sibling,
            )
        )
        w_sib.append(
            sems.copy(
                lambda u=u: wout.at[span(u), pl.ds(mine, 64), :],
                lambda u=u: wout.at[span(u), pl.ds(mine, 64), :],
                me.sibling,
            )
        )
        w_out.append(
            pltpu.make_async_copy(wout.at[span(u)], wout_hbm.at[span(u)], store_sem.at[u])
        )
        w_a.append([
            sems.copy(
                lambda h=h, d=d: wpart.at[h, pl.ds(row_a(h, d), 16), :],
                lambda h=h, d=d: ra.at[d - 1, h],
                lambda h=h, d=d: me.along(ORDERS[h][0], d),
            )
            for h in heads(u) for d in range(1, 4)
        ])
        w_b.append([
            sems.copy(
                lambda h=h, d=d: sa.at[h, :, pl.ds(col_b(h, d), 512)],
                lambda h=h, d=d: rb.at[d - 1, h],
                lambda h=h, d=d: me.along(ORDERS[h][1], d),
            )
            for h in heads(u) for d in range(1, 4)
        ])
        w_c.append([
            sems.copy(
                lambda h=h, d=d: sb.at[h, :, pl.ds(col_c(h, d), 128)],
                lambda h=h, d=d: rc.at[d - 1, h],
                lambda h=h, d=d: me.along(ORDERS[h][2], d),
            )
            for h in heads(u) for d in range(1, 4)
        ])
        for step in range(3):
            w_g[step].append([
                sems.copy(
                    lambda h=h, step=step: piece(h, step),
                    lambda h=h, step=step: piece(h, step),
                    lambda h=h, d=d, step=step: me.along(ORDERS[h][step], d),
                )
                for h in heads(u) for d in range(1, 4)
            ])

    def weigh(u):
        def some(i, carry):
            c = pl.ds(pl.multiple_of(i * 512, 512), 512)
            part = dot(att[columns(u), :], go_ref[:, c], 1, 0)
            wpart[span(u), :, c] = part.reshape(UNITS[u][1], WIDTH, 512).astype(BF)
            return carry

        lax.fori_loop(0, COLS // 512, some, 0)
        w_core[u].start()

    def weight_core(u):
        w_core[u].wait()

        def some(h, carry):
            r = pl.ds(mine, 64)
            wpart[h, r, :] = (wpart[h, r, :].astype(F32) + wr0[h].astype(F32)).astype(BF)
            return carry

        lax.fori_loop(heads(u)[0], heads(u)[-1] + 1, some, 0)
        start(w_a[u])

    def weight_a(u):
        wait(w_a[u])
        for h in heads(u):
            t = wpart[h, pl.ds(row_a(h), 16), :].astype(F32)
            for d in range(3):
                t = t + ra[d, h].astype(F32)
            sa[h] = t.astype(BF)
        start(w_b[u])

    def weight_b(u):
        wait(w_b[u])
        for h in heads(u):
            t = sa[h, :, pl.ds(col_b(h), 512)].astype(F32)
            for d in range(3):
                t = t + rb[d, h].astype(F32)
            sb[h] = t.astype(BF)
        start(w_c[u])

    def weight_c(u):
        wait(w_c[u])
        for h in heads(u):
            t = sb[h, :, pl.ds(col_c(h), 128)].astype(F32)
            for d in range(3):
                t = t + rc[d, h].astype(F32)
            wout[h, pl.ds(row_a(h), 16), pl.ds(col_bc(h), 128)] = t.astype(BF)
        start(w_g[2][u])

    def weight_gather(u, step):
        wait(w_g[step][u])
        if step > 0:
            start(w_g[step - 1][u])
        else:
            w_sib[u].start()

    def weight_last(u):
        w_sib[u].wait()
        w_out[u].start()

    n_core, n_z, n_x, n_y = [], [], [], []
    for u in range(3):
        n_core.append(
            sems.copy(
                lambda u=u: gnf.at[:, pl.ds(HALF, HALF), columns(u)],
                lambda u=u: cr.at[:, :, columns(u)],
                me.sibling,
            )
        )
        n_z.append([
            sems.copy(
                lambda u=u, d=d: near_snd.at[:, :, d, :, columns(u)],
                lambda u=u, d=d: zr.at[d, :, :, :, columns(u)],
                lambda d=d: me.along(2, d),
            )
            for d in range(1, 4)
        ])
        n_x.append(
            sems.copy(
                lambda u=u: xs.at[:, :, columns(u)],
                lambda u=u: xr.at[:, :, columns(u)],
                lambda: me.chip(4),
            )
        )
        n_y.append([
            sems.copy(
                lambda u=u, d=d: far_snd.at[:, pl.ds(32 * d, 32), columns(u)],
                lambda u=u, d=d: yr.at[d, :, :, columns(u)],
                lambda d=d: me.along(1, d),
            )
            for d in range(1, 4)
        ])
    own_reduce = [
        sems.copy(lambda m=m: bxs.at[m], lambda m=m: bxr.at[m], lambda m=m: me.cross(m))
        for m in range(1, 16)
    ]

    def near_core(u):
        n_core[u].wait()
        cs = columns(u)
        for i in range(2):
            t = (gnf[i, 0:HALF, cs].astype(F32) + cr[i, :, cs].astype(F32)).astype(BF)
            for c in range(CHIPS):
                near_snd[i, c // 4, c % 4, :, cs] = t[32 * c : 32 * c + 32]
            far_snd[i, :, cs] = t[FAR:]
        start(n_z[u])
        start(n_y[u])

    def near_z(u):
        wait(n_z[u])
        cs = columns(u)
        for i in range(2):
            for x in range(2):
                t = near_snd[i, x, 0, :, cs].astype(F32)
                for d in range(1, 4):
                    t = t + zr[d, i, x, :, cs].astype(F32)
                if x == 0:
                    tot[i, :, cs] = t
                else:
                    xs[i, :, cs] = t.astype(BF)
        n_x[u].start()

    def near_x(u):
        n_x[u].wait()
        cs = columns(u)
        for i in range(2):
            tot[i, :, cs] = (tot[i, :, cs] + xr[i, :, cs].astype(F32)) * (1.0 / S1)

    def near_y(u):
        wait(n_y[u])
        cs = columns(u)
        for i in range(2):
            t = far_snd[i, 0:32, cs].astype(F32)
            for d in range(1, 4):
                t = t + yr[d, i, :, cs].astype(F32)
            xblk[i, :, cs] = t
        for part in ((), (0, 1, 2), (3,))[u]:
            for m in range(16):
                for i in range(2):
                    packed[m, 4 * part + 2 * i : 4 * part + 2 * i + 2, :] = xblk[
                        i, 2 * m : 2 * m + 2, part * 256 : part * 256 + 256
                    ]
        if u == 2:
            bxs[...] = packed[...].astype(BF)
            start(own_reduce)

    def finish_rows():
        wait(own_reduce)
        t = bxs[0].astype(F32)
        for m in range(1, 16):
            t = t + bxr[m].astype(F32)
        t = t * (1.0 / (S1 * S1))
        for i in range(2):
            for r in range(2):
                far_row = jnp.concatenate(
                    [t[4 * p + 2 * i + r : 4 * p + 2 * i + r + 1] for p in range(4)], axis=1
                )
                tot[i, 16 * r : 16 * r + 16, :] = tot[i, 16 * r : 16 * r + 16, :] + far_row

        def some(i, carry):
            r = pl.ds(pl.multiple_of(i * S1, S1), S1)
            k_ref[r, :] = (fine_k[r, :] + tot[0, pl.ds(i, 1), :]).astype(BF)
            v_ref[r, :] = (fine_v[r, :] + tot[1, pl.ds(i, 1), :]).astype(BF)
            return carry

        lax.fori_loop(0, ROWS // S1, some, 0, unroll=2)

    pair_row = lax.broadcasted_iota(jnp.int32, (32, ROWS), 0) // S1
    pair_col = lax.broadcasted_iota(jnp.int32, (32, ROWS), 1) // PAIR
    own_pair = pair_row == pair_col

    def forward(h):
        c = pl.ds(pl.multiple_of(h * WIDTH, WIDTH), WIDTH)
        qh = q_ref[:, c]
        s = dot(nf[0, :, c], qh, 1, 1)
        sf = [
            dot(k_ref[p * PAIR : (p + 1) * PAIR, c], qh[p * PAIR : (p + 1) * PAIR], 1, 1)
            for p in range(2)
        ]
        sf = jnp.concatenate(sf, axis=1)
        top = jnp.maximum(jnp.max(s, axis=0, keepdims=True), jnp.max(sf, axis=0, keepdims=True))
        e = jnp.exp2((s - top) * EXP2_SCALE)
        none = jnp.zeros((16, ROWS), F32)
        e = jnp.concatenate(
            [
                jnp.where(own_pair, 0.0, e[0:32]),
                e[32:FAR],
                none,
                e[FAR + 16 : HALF + FAR],
                none,
                e[HALF + FAR + 16 :],
            ],
            axis=0,
        )
        ef = jnp.exp2((sf - top) * EXP2_SCALE)
        total = jnp.sum(e, axis=0, keepdims=True) + jnp.sum(ef, axis=0, keepdims=True)
        e = e.astype(BF)
        ef = ef.astype(BF)
        probs[h, 0:KEYS, :] = e
        probs[h, KEYS : KEYS + PAIR, :] = ef
        out = dot(nf[1, :, c], e, 0, 0)
        of = [
            dot(v_ref[p * PAIR : (p + 1) * PAIR, c], ef[:, p * PAIR : (p + 1) * PAIR], 0, 0)
            for p in range(2)
        ]
        out = out + jnp.concatenate(of, axis=1)
        inv = 1.0 / total
        out = (out * inv).astype(BF)
        att[c, :] = out
        gth = gt[c, :].astype(F32)
        d = jnp.sum(out.astype(F32) * gth, axis=0, keepdims=True) * inv
        delta[h] = jnp.broadcast_to(d, (8, ROWS))
        scaled = gth * inv
        gst[c, :] = scaled.astype(BF)
        gs[:, c] = scaled.T.astype(BF)

    def backward(h):
        c = pl.ds(pl.multiple_of(h * WIDTH, WIDTH), WIDTH)
        qh = q_ref[:, c]
        gth = gst[c, :]
        gh = gs[:, c]
        d = delta[h, 0:1, :]
        e = probs[h, 0:KEYS, :]
        ds = (e.astype(F32) * (dot(nf[1, :, c], gth, 1, 0) - d)).astype(BF)
        gnf[1, :, c] = dot(e, gh, 1, 0).astype(BF)
        gnf[0, :, c] = (dot(ds, qh, 1, 0) * SCALE).astype(BF)
        dq = dot(nf[0, :, c], ds, 0, 0)
        dqf = []
        for p in range(2):
            r = slice(p * PAIR, (p + 1) * PAIR)
            ef = probs[h, KEYS : KEYS + PAIR, r]
            dsf = (ef.astype(F32) * (dot(v_ref[r, c], gth[:, r], 1, 0) - d[:, r])).astype(BF)
            fine_v[r, c] = dot(ef, gh[r], 1, 0)
            fine_k[r, c] = dot(dsf, qh[r], 1, 0) * SCALE
            dqf.append(dot(k_ref[r, c], dsf, 0, 0))
        dq = (dq + jnp.concatenate(dqf, axis=1)) * SCALE
        q_ref[:, c] = dq.T.astype(BF)

    def scheduled(work, plan):
        def step(h, carry):
            work(h)
            for at, actions in plan.items():

                @pl.when(h == at)
                def _():
                    for action, *args in actions:
                        action(*args)

            return carry

        lax.fori_loop(0, HEADS, step, 0)

    def near_send(u):
        n_core[u].start()

    scheduled(
        forward,
        {
            1: [(gather_near, 1)],
            2: [(gather_far, 1), (weigh, 0)],
            3: [(weight_core, 0)],
            4: [(gather_near, 2)],
            5: [(gather_far, 2), (weigh, 1)],
            6: [(weight_core, 1)],
            7: [(weight_a, 0), (weigh, 2)],
        },
    )
    scheduled(
        backward,
        {
            0: [(weight_core, 2)],
            1: [(weight_a, 1), (weight_b, 0)],
            2: [(near_send, 0)],
            3: [(weight_c, 0), (weight_a, 2), (weight_b, 1), (near_core, 0)],
            5: [(near_send, 1), (weight_gather, 0, 2), (weight_c, 1), (weight_b, 2)],
            6: [(near_core, 1)],
            7: [
                (near_send, 2), (weight_gather, 0, 1), (weight_gather, 1, 2), (weight_c, 2),
                (near_z, 0),
            ],
        },
    )
    store_q = pltpu.make_async_copy(q_ref, gq_hbm, store_sem.at[3])
    store_q.start()
    near_core(2)
    weight_gather(2, 2)
    weight_gather(1, 1)
    near_y(0)
    near_z(1)
    near_y(1)
    weight_gather(2, 1)
    near_y(2)
    weight_gather(0, 0)
    near_z(2)
    near_x(0)
    near_x(1)
    weight_gather(1, 0)
    near_x(2)
    finish_rows()
    store_k = pltpu.make_async_copy(k_ref, gk_hbm, store_sem.at[4])
    store_v = pltpu.make_async_copy(v_ref, gv_hbm, store_sem.at[5])
    store_k.start()
    store_v.start()
    weight_last(0)
    weight_last(1)
    weight_gather(2, 0)
    weight_last(2)
    for copy in w_out + [store_q, store_k, store_v]:
        copy.wait()


def finish(
    scale, gq_in, gk_in, gv_in, w_in, gq_out, gk_out, gv_out, w_out,
    part, wide, kept, in_sem, out_sem,
):
    ins = [pltpu.make_async_copy(w_in.at[h], part.at[h], in_sem.at[h]) for h in range(HEADS)]
    outs = [
        pltpu.make_async_copy(wide.at[h], w_out.at[pl.ds(h * WIDTH, WIDTH)], out_sem.at[h])
        for h in range(HEADS)
    ]
    for i, (src, dst) in enumerate(((gq_in, gq_out), (gk_in, gk_out), (gv_in, gv_out))):
        ins.append(pltpu.make_async_copy(src, kept.at[i], in_sem.at[HEADS + i]))
        outs.append(pltpu.make_async_copy(kept.at[i], dst, out_sem.at[HEADS + i]))
    for copy in ins:
        copy.start()
    for h in range(HEADS):
        ins[h].wait()
        wide[h] = part[h].astype(F32) * scale
        outs[h].start()
    for i in range(HEADS, HEADS + 3):
        ins[i].wait()
        outs[i].start()
    for copy in outs:
        copy.wait()


def body(queries, key_rows, value_rows, grad_output, out_weight):
    vmem = pltpu.VMEM
    dma = pltpu.SemaphoreType.DMA
    scratch = [
        vmem((ROWS, ALL), BF),
        vmem((ROWS, ALL), BF),
        vmem((ROWS, ALL), BF),
        vmem((ROWS, COLS), BF),
        vmem((ALL, COLS), BF),
        vmem((2, KEYS, ALL), BF),
        vmem((16, 256), BF),
        vmem((16, 16, 256), BF),
        vmem((2, 32, ALL), F32),
        vmem((ALL, ROWS), BF),
        vmem((ALL, ROWS), BF),
        vmem((HEADS, KEYS + PAIR, ROWS), BF),
        vmem((ALL, ROWS), BF),
        vmem((ROWS, ALL), BF),
        vmem((HEADS, 8, ROWS), F32),
        vmem((2, KEYS, ALL), BF),
        vmem((2, HALF, ALL), BF),
        vmem((2, 2, 4, 32, ALL), BF),
        vmem((2, 128, ALL), BF),
        vmem((4, 2, 2, 32, ALL), BF),
        vmem((2, 32, ALL), BF),
        vmem((2, 32, ALL), BF),
        vmem((4, 2, 32, ALL), BF),
        vmem((16, 16, 256), F32),
        vmem((16, 16, 256), BF),
        vmem((16, 16, 256), BF),
        vmem((ROWS, ALL), F32),
        vmem((ROWS, ALL), F32),
        vmem((2, 32, ALL), F32),
        vmem((HEADS, WIDTH, COLS), BF),
        vmem((HEADS, 64, COLS), BF),
        vmem((3, HEADS, 16, COLS), BF),
        vmem((3, HEADS, 16, 512), BF),
        vmem((3, HEADS, 16, 128), BF),
        vmem((HEADS, 16, COLS), BF),
        vmem((HEADS, 16, 512), BF),
        vmem((HEADS, WIDTH, COLS), BF),
        dma((5,)),
        dma((6,)),
        dma((NSEM,)),
        dma((NSEM,)),
    ]
    hbm = pl.BlockSpec(memory_space=pl.ANY)
    token_shape = jax.ShapeDtypeStruct((ROWS, ALL), BF)
    grads = pl.pallas_call(
        kernel,
        out_shape=(token_shape,) * 3 + (jax.ShapeDtypeStruct((HEADS, WIDTH, COLS), BF),),
        in_specs=[hbm] * 5,
        out_specs=(hbm,) * 4,
        scratch_shapes=scratch,
        compiler_params=pltpu.CompilerParams(
            collective_id=0, has_side_effects=True, vmem_limit_bytes=64 * 1024 * 1024 - 65536
        ),
        name="fused",
    )(queries, key_rows, value_rows, grad_output, out_weight)
    tokens = ROWS * lax.axis_size("node") * lax.axis_size("group")
    return pl.pallas_call(
        functools.partial(finish, 1.0 / math.sqrt(tokens)),
        out_shape=(token_shape,) * 3 + (jax.ShapeDtypeStruct((ALL, COLS), F32),),
        in_specs=[hbm] * 4,
        out_specs=(hbm,) * 4,
        scratch_shapes=[
            vmem((HEADS, WIDTH, COLS), BF),
            vmem((HEADS, WIDTH, COLS), F32),
            vmem((3, ROWS, ALL), BF),
            dma((HEADS + 3,)),
            dma((HEADS + 3,)),
        ],
        compiler_params=pltpu.CompilerParams(vmem_limit_bytes=64 * 1024 * 1024 - 65536),
        name="finish",
    )(*grads)


def solution(mesh):
    split = P(("group", "node"), None)
    return jax.shard_map(
        body,
        mesh=mesh,
        in_specs=(split, split, split, split, P()),
        out_specs=(split, split, split, P()),
        check_vma=False,
    )
```
